32 devices in a mesh: rows: 16 (over z, y, core), cols: 2 (over x).
Axes of the slice: x: 2, y: 2, z: 4, core: 2. Of those that a mesh axis runs over, the one named last changes fastest.
Arguments:
- patches: bfloat16 [128, 128, 512], P('rows', 'cols'), may hold values from -6 to 6
- tissue: int32 [128, 128], P('rows', 'cols'), may hold values 0 or 1
- w_value: bfloat16 [512, 512], replicated, may hold values from -0.25 to 0.25
- w_across: bfloat16 [512, 40], replicated, may hold values from -0.25 to 0.25
- w_down: bfloat16 [512, 40], replicated, may hold values from -0.25 to 0.25
- w_gate: bfloat16 [512, 512], replicated, may hold values from -0.25 to 0.25
- w_out: bfloat16 [512, 512], replicated, may hold values from -0.25 to 0.25
- step_bias_across: float32 [8], replicated, may hold values from -4.5 to -2.5
- step_bias_down: float32 [8], replicated, may hold values from -4.5 to -2.5
- rates_across: float32 [8], replicated, may hold values from 0.015625 to 1
- rates_down: float32 [8], replicated, may hold values from 0.015625 to 1
- skip_across: float32 [8], replicated, may hold values from 0.5 to 1.5
- skip_down: float32 [8], replicated, may hold values from 0.5 to 1.5
- gain_across: float32 [512], replicated, may hold values from 0.5 to 1.5
- gain_final: float32 [512], replicated, may hold values from 0.5 to 1.5
Outputs:
- mixed: bfloat16 [128, 128, 512], P('rows', 'cols')
The draws below stay inside these ranges and needn't reach their ends.
Inputs may be any that keep to these rules, and one draw needn't show every extreme that they name: 1 marks a tissue patch, 0 background.
All inputs are finite; a program needn't handle non-finite values. No bound on the sum of `tissue` on one device may be relied on, other than what follows from the above.
Results may differ from the reference program's by a relative error of at most 0.015.
Values may be sent and summed in bfloat16 or wider, within the bound.
A program may use at most 64 MiB of HBM per device.

```python
import math
import jax
import jax.numpy as jnp
from jax import lax

HEADS = 8
D = 512
PROJ = 40
H = 128
W = 128


def set_ends(result, rng, low, high):
    longest = result.shape.index(max(result.shape))
    spots = []
    for shift in (0, 1):
        where = [jax.random.randint(jax.random.fold_in(rng, axis), (), 0, length) for axis, length in enumerate(result.shape)]
        where[longest] = (where[longest] + shift) % result.shape[longest]
        spots.append(tuple(where))
    return result.at[spots[0]].set(low).at[spots[1]].set(high)


def level_of(key, extent, shards, smallest, high):
    def one(dim, shards_of):
        draws = jax.random.uniform(jax.random.fold_in(jax.random.fold_in(key, 6), dim), (shards_of,), jnp.float32, smallest / len(shards), high / len(shards))
        return jnp.repeat(jnp.exp(draws), extent[dim] // shards_of).reshape((-1,) + (1,) * (len(extent) - dim - 1))

    factor_of = one(*shards[0])
    for cut in shards[1:]:
        factor_of = factor_of * one(*cut)
    return factor_of


def scatter_about(stream_key, dims, width, bound, split=(), dtype=jnp.bfloat16):
    entries = width * jax.random.normal(stream_key, dims, jnp.float32)
    if split:
        entries = entries * level_of(stream_key, dims, split, -0.22, 0.18)
    return jnp.clip(entries, -bound, bound).astype(dtype)


def setup_inputs(seed: int = 0) -> dict:
    streams_of = jax.random.split(jax.random.key(seed), 16)
    return {
        "patches": scatter_about(streams_of[0], (H, W, D), 1.0, 6.0, ((0, 16), (1, 2))),
        "tissue": set_ends((jax.random.randint(streams_of[1], (H, W), 0, 4) < 3).astype(jnp.int32), jax.random.fold_in(streams_of[1], 1), 0, 1),
        "w_value": scatter_about(streams_of[2], (D, D), D ** -0.5, 0.25),
        "w_across": scatter_about(streams_of[3], (D, PROJ), D ** -0.5, 0.25),
        "w_down": scatter_about(streams_of[4], (D, PROJ), D ** -0.5, 0.25),
        "w_gate": scatter_about(streams_of[5], (D, D), D ** -0.5, 0.25),
        "w_out": scatter_about(streams_of[6], (D, D), D ** -0.5, 0.25),
        "step_bias_across": jnp.clip(jax.random.uniform(streams_of[7], (HEADS,), jnp.float32, -4.5, -2.5), -4.5, -2.5),
        "step_bias_down": jnp.clip(jax.random.uniform(streams_of[8], (HEADS,), jnp.float32, -4.5, -2.5), -4.5, -2.5),
        "rates_across": jnp.clip(jnp.exp(jax.random.uniform(streams_of[9], (HEADS,), jnp.float32, math.log(0.015625), math.log(1.0))), 0.015625, 1.0),
        "rates_down": jnp.clip(jnp.exp(jax.random.uniform(streams_of[10], (HEADS,), jnp.float32, math.log(0.015625), math.log(1.0))), 0.015625, 1.0),
        "skip_across": jnp.clip(jax.random.uniform(streams_of[11], (HEADS,), jnp.float32, 0.5, 1.5), 0.5, 1.5),
        "skip_down": jnp.clip(jax.random.uniform(streams_of[12], (HEADS,), jnp.float32, 0.5, 1.5), 0.5, 1.5),
        "gain_across": jnp.clip(1.0 + 0.1 * jax.random.normal(streams_of[13], (D,), jnp.float32), 0.5, 1.5),
        "gain_final": jnp.clip(1.0 + 0.1 * jax.random.normal(streams_of[14], (D,), jnp.float32), 0.5, 1.5),
    }


highest = lax.Precision.HIGHEST

def rounded(values):
    return lax.optimization_barrier(values.astype(jnp.bfloat16)).astype(jnp.float32)

def scan_parts(values, b_rows, c_rows, step_sizes, rates, skips):
    line_count, length, head_count, head_width = values.shape
    state_count = b_rows.shape[-1]
    block_len = math.gcd(length, 128)
    block_count = length // block_len
    inputs = values.astype(jnp.float32).reshape(line_count, block_count, block_len, head_count, head_width)
    b_blocks = b_rows.reshape(line_count, block_count, block_len, state_count)
    c_blocks = c_rows.reshape(line_count, block_count, block_len, state_count)
    step_blocks = step_sizes.reshape(line_count, block_count, block_len, head_count)
    running = jnp.cumsum(-step_blocks * rates, axis=2)
    causal = (jnp.arange(block_len)[:, None] >= jnp.arange(block_len)[None, :])[None, None, :, :, None]
    spans = jnp.where(causal, running[:, :, :, None, :] - running[:, :, None, :, :], 0.0)
    decays = jnp.where(causal, jnp.exp(spans), 0.0)
    intersections = jnp.einsum('lctn,lcsn->lcts', c_blocks, b_blocks, precision=highest)
    weights = rounded(decays * intersections[..., None] * step_blocks[:, :, None, :, :])
    within = jnp.einsum('lctsh,lcshp->lcthp', weights, inputs, precision=highest)
    to_end = jnp.exp(running[:, :, -1:, :] - running) * step_blocks
    push_coef = rounded(b_blocks[..., :, None] * to_end[..., None, :])
    pushed = jnp.einsum('lcsnh,lcshp->lchnp', push_coef, inputs, precision=highest)
    totals = running[:, :, -1, :]

    def advance(entered, item):
        pushed_one, total_one = item
        return (jnp.exp(total_one)[..., None, None] * entered + pushed_one, entered)
    final, entering = lax.scan(advance, jnp.zeros_like(pushed[:, 0]), (jnp.moveaxis(pushed, 1, 0), jnp.moveaxis(totals, 1, 0)))
    entering = jnp.moveaxis(entering, 0, 1)
    carried = jnp.einsum('lctn,lchnp->lcthp', c_blocks, entering, precision=highest) * jnp.exp(running)[..., None]
    outputs = within + carried + skips[:, None] * inputs
    return outputs.reshape(line_count, length, head_count * head_width)

def line_scan(values, projected, step_bias, rates, skips):
    head_count = rates.shape[0]
    state_count = (projected.shape[-1] - head_count) // 2
    line_count, length, width_all = values.shape
    b_rows = projected[..., :state_count]
    c_rows = projected[..., state_count:2 * state_count]
    step_sizes = jax.nn.softplus(projected[..., 2 * state_count:] + step_bias)
    return scan_parts(values.reshape(line_count, length, head_count, width_all // head_count), b_rows, c_rows, step_sizes, rates, skips)

def rms_norm(values, gain):
    return values * lax.rsqrt(lax.optimization_barrier(jnp.mean(values * values, axis=-1, keepdims=True)) + 1e-05) * gain

def reference(patches, tissue, w_value, w_across, w_down, w_gate, w_out, step_bias_across, step_bias_down, rates_across, rates_down, skip_across, skip_down, gain_across, gain_final):
    masked = patches * tissue.astype(jnp.bfloat16)[..., None]
    row_total, col_total, feature_count = masked.shape
    row_group = math.gcd(row_total, 16)

    def across(row_block):
        values_across = jnp.dot(row_block, w_value, preferred_element_type=jnp.float32).astype(jnp.bfloat16)
        proj_across = jnp.dot(row_block, w_across, preferred_element_type=jnp.float32)
        y_across = line_scan(values_across, proj_across, step_bias_across, rates_across, skip_across)
        return rms_norm(y_across, gain_across).astype(jnp.bfloat16)
    line_out = lax.map(across, masked.reshape(row_total // row_group, row_group, col_total, feature_count)).reshape(masked.shape)
    columns = jnp.swapaxes(line_out, 0, 1)
    col_group = math.gcd(col_total, 8)

    def downward(col_block):
        proj_down = jnp.dot(col_block, w_down, preferred_element_type=jnp.float32)
        y_down = line_scan(col_block, proj_down, step_bias_down, rates_down, skip_down)
        return y_down.astype(jnp.bfloat16)
    column_out = lax.map(downward, columns.reshape(col_total // col_group, col_group, row_total, feature_count))
    column_out = jnp.swapaxes(column_out.reshape(col_total, row_total, feature_count), 0, 1)
    gate = jnp.dot(masked, w_gate, preferred_element_type=jnp.float32)
    act = (rms_norm(column_out.astype(jnp.float32), gain_final) * jax.nn.silu(gate)).astype(jnp.bfloat16)
    return (masked.astype(jnp.float32) + jnp.dot(act, w_out, preferred_element_type=jnp.float32)).astype(jnp.bfloat16)
```

```python
import functools

import jax
import jax.numpy as jnp
from jax import lax
from jax.experimental import pallas as pl
from jax.experimental.pallas import tpu as pltpu
from jax.sharding import PartitionSpec as P

MESH = pl.DeviceIdType.MESH
f32 = jnp.float32
bf16 = jnp.bfloat16


def mm(a, b):
    return jnp.dot(a, b, preferred_element_type=f32)


def mm_nt(a, b):
    return lax.dot_general(a, b, (((1,), (1,)), ((), ())), preferred_element_type=f32)


def mm_tn(a, b):
    return lax.dot_general(a, b, (((0,), (0,)), ((), ())), preferred_element_type=f32)


def parts_of(x):
    high = x.astype(bf16)
    return high, (x - high.astype(f32)).astype(bf16)


def mm_split_right(a, x):
    high, low = parts_of(x)
    return mm(a, high) + mm(a, low)


def mm_split_left(x, b):
    high, low = parts_of(x)
    return mm(high, b) + mm(low, b)


def iota(shape, dim):
    return lax.broadcasted_iota(jnp.int32, shape, dim)


def log2_of(size):
    assert size & (size - 1) == 0
    return size.bit_length() - 1


def one_hot(count, index):
    return jnp.where(iota((count, count), 1) == index, 1.0, 0.0).astype(bf16)


def block_kernel(
    n_rows,
    n_cols,
    patches_ref,
    tissue_ref,
    w_value_ref,
    w_across_ref,
    w_down_ref,
    w_gate_ref,
    w_out_ref,
    bias_a_ref,
    bias_d_ref,
    rates_a_ref,
    rates_d_ref,
    skip_a_ref,
    skip_d_ref,
    gain_a_ref,
    gain_f_ref,
    out_ref,
    masked,
    vals,
    b_all,
    c_all,
    s_exp,
    l_exp,
    y_all,
    gated,
    pushed_all,
    l_end,
    state_out,
    state_in,
    send1,
    recv1,
    send2,
    recv2,
    send_sems,
    recv_sems,
    relay_sems,
):
    local_rows, width, feats = patches_ref.shape
    heads = rates_a_ref.shape[1]
    head_width = feats // heads
    states = (w_across_ref.shape[1] - heads) // 2
    tokens = local_rows * width
    chunk = width
    chunks = tokens // chunk
    per_peer = width // n_rows
    height = n_rows * local_rows
    assert head_width == chunk and height % chunk == 0

    my_row = lax.axis_index("rows")
    my_col = lax.axis_index("cols")

    barrier = pltpu.get_barrier_semaphore()

    @pl.loop(1, n_rows)
    def _(off):
        pl.semaphore_signal(
            barrier,
            inc=1,
            device_id=(lax.rem(my_row + off, n_rows), my_col),
            device_id_type=MESH,
        )

    @pl.when(my_col > 0)
    def _():
        pl.semaphore_signal(
            barrier, inc=1, device_id=(my_row, my_col - 1), device_id_type=MESH
        )

    lane = iota((heads, feats), 1)
    first = iota((heads, feats), 0) * head_width
    expand = jnp.where((lane >= first) & (lane < first + head_width), 1.0, 0.0).astype(bf16)
    place_t = iota((chunk, feats), 0)
    place_u = iota((chunk, feats), 1) & (head_width - 1)
    causal = place_t >= place_u
    diagonal = place_t == place_u
    tri = jnp.where(iota((chunk, chunk), 0) >= iota((chunk, chunk), 1), 1.0, 0.0).astype(bf16)
    group = min(heads, 4)
    gw = group * head_width
    sh = log2_of(head_width)
    same_head = jnp.where(
        lax.shift_right_logical(iota((gw, gw), 0), sh)
        == lax.shift_right_logical(iota((gw, gw), 1), sh),
        1.0,
        0.0,
    ).astype(bf16)

    def wide(ref):
        return mm_split_left(jnp.broadcast_to(ref[...], (8, heads)), expand)[0:1]

    def project(x, w_ref, bias_ref):
        proj = mm(x, w_ref[...])
        b_all[...] = proj[:, :states].astype(bf16)
        c_all[...] = proj[:, states : 2 * states].astype(bf16)
        v = proj[:, 2 * states :] + bias_ref[...]
        steps = jnp.maximum(v, 0.0) + jnp.log1p(jnp.exp(-jnp.abs(v)))
        s_exp[...] = mm_split_left(steps, expand)

    def push(g, neg_rates):
        rows = pl.ds(pl.multiple_of(g * chunk, chunk), chunk)
        s = s_exp[rows, :]
        run = mm_split_right(tri, s * neg_rates)
        end = run[chunk - 1 : chunk, :]
        v = vals[rows, :].astype(f32)
        pushed = mm_tn(b_all[rows, :], (v * (jnp.exp(end - run) * s)).astype(bf16))
        return rows, s, run, end, v, pushed

    def within(rows, s, run, v, skips):
        run_u = jnp.sum(jnp.where(diagonal, run, 0.0), axis=0, keepdims=True)
        s_u = jnp.sum(jnp.where(diagonal, s, 0.0), axis=0, keepdims=True)
        b = b_all[rows, :]
        cb = mm_nt(c_all[rows, :], jnp.concatenate([b] * heads, axis=0))
        decay = jnp.exp(jnp.where(causal, run - run_u, -1e30))
        weights = (decay * cb * s_u).astype(bf16)
        vb = v.astype(bf16)
        outs = []
        for q in range(heads // group):
            lanes = slice(q * gw, (q + 1) * gw)
            stacked = jnp.concatenate([vb[:, lanes]] * group, axis=0) * same_head
            outs.append(mm(weights[:, lanes], stacked))
        return jnp.concatenate(outs, axis=1) + skips * v

    def exchange(slot, source, target):
        def copy_of(off):
            to = lax.rem(my_row + off, n_rows)
            return pltpu.make_async_remote_copy(
                src_ref=source.at[to],
                dst_ref=target.at[my_row],
                send_sem=send_sems.at[slot, off],
                recv_sem=recv_sems.at[slot, off],
                device_id=(to, my_col),
                device_id_type=MESH,
            )

        def start():
            @pl.loop(1, n_rows)
            def _(off):
                copy_of(off).start()

            target[my_row] = source[my_row]

        def finish():
            @pl.loop(1, n_rows)
            def _(off):
                came = lax.rem(my_row + n_rows - off, n_rows)
                pltpu.make_async_remote_copy(
                    src_ref=source.at[came],
                    dst_ref=target.at[came],
                    send_sem=send_sems.at[slot, off],
                    recv_sem=recv_sems.at[slot, off],
                    device_id=(came, my_col),
                    device_id_type=MESH,
                ).wait_recv()

        def drain():
            @pl.loop(1, n_rows)
            def _(off):
                copy_of(off).wait_send()

        return start, finish, drain

    def put(ref, x):
        if ref.shape[1] % 16:
            x = x.astype(f32).reshape(ref.shape).astype(bf16)
        else:
            x = x.astype(bf16).reshape(ref.shape)
        ref[...] = x

    def take(ref):
        x = ref[...]
        if ref.shape[1] % 16:
            return x.astype(f32).reshape(tokens, feats).astype(bf16)
        return x.reshape(tokens, feats)

    flags = tissue_ref[...].astype(f32).T
    for r in range(local_rows):
        flag = jnp.broadcast_to(flags[:, r : r + 1], (width, feats)) > 0.5
        masked[r * width : (r + 1) * width, :] = jnp.where(
            flag, patches_ref[r].astype(f32), 0.0
        ).astype(bf16)

    x = masked[...]
    vals[...] = mm(x, w_value_ref[...]).astype(bf16)
    project(x, w_across_ref, bias_a_ref)
    neg_rates = -wide(rates_a_ref)
    skips = wide(skip_a_ref)

    @pl.loop(0, chunks)
    def _(g):
        rows, _, run, end, _, pushed = push(g, neg_rates)
        l_exp[rows, :] = run
        l_end[g] = end
        pushed_all[g] = pushed

    greeted = n_rows - 1 + jnp.where(my_col < n_cols - 1, 1, 0)
    pl.semaphore_wait(barrier, greeted)

    relay = pltpu.make_async_remote_copy(
        src_ref=state_out,
        dst_ref=state_in,
        send_sem=relay_sems.at[0],
        recv_sem=relay_sems.at[1],
        device_id=(my_row, lax.rem(my_col + 1, n_cols)),
        device_id_type=MESH,
    )

    @pl.when(my_col == 0)
    def _():
        state_in[...] = jnp.zeros_like(state_in)
        if n_cols > 1:
            state_out[...] = pushed_all[...].astype(bf16)
            relay.start()

    @pl.loop(0, chunks)
    def _(g):
        rows = pl.ds(pl.multiple_of(g * chunk, chunk), chunk)
        y_all[rows, :] = within(
            rows, s_exp[rows, :], l_exp[rows, :], vals[rows, :].astype(f32), skips
        )

    @pl.when(my_col > 0)
    def _():
        relay.wait_recv()

        @pl.when(my_col < n_cols - 1)
        def _():
            state_out[...] = (
                pushed_all[...] + jnp.exp(l_end[...]) * state_in[...].astype(f32)
            ).astype(bf16)
            relay.start()

    gain_a = gain_a_ref[...]

    @pl.loop(0, chunks)
    def _(g):
        rows = pl.ds(pl.multiple_of(g * chunk, chunk), chunk)
        y = y_all[rows, :] + mm(c_all[rows, :], state_in[g]) * jnp.exp(l_exp[rows, :])
        scale = lax.rsqrt(jnp.mean(y * y, axis=-1, keepdims=True) + 1e-5)
        vals[rows, :] = (y * scale * gain_a).astype(bf16)

    rsh = log2_of(local_rows)
    csh = log2_of(width)
    m = iota((tokens, tokens), 0)
    by_col = one_hot(
        tokens,
        ((m & (local_rows - 1)) << csh) + lax.shift_right_logical(m, rsh),
    )
    put(send1, mm(by_col, vals[...]))
    start1, finish1, drain1 = exchange(0, send1, recv1)
    start1()

    gate = mm(masked[...], w_gate_ref[...])
    gated[...] = gate / (1.0 + jnp.exp(-gate)) * gain_f_ref[...]
    neg_rates_d = -wide(rates_d_ref)
    skips_d = wide(skip_d_ref)
    hsh = log2_of(height)
    psh = log2_of(per_peer)
    m = iota((tokens, tokens), 0)
    c_of = lax.shift_right_logical(m, hsh)
    i_of = m & (height - 1)
    to_columns = one_hot(
        tokens,
        (lax.shift_right_logical(i_of, rsh) << (rsh + psh))
        + (c_of << rsh)
        + (i_of & (local_rows - 1)),
    )

    @pl.when(my_col < n_cols - 1)
    def _():
        relay.wait_send()

    finish1()
    cols = mm(to_columns, take(recv1)).astype(bf16)
    vals[...] = cols
    project(cols, w_down_ref, bias_d_ref)

    per_line = height // chunk

    def line(c, _):
        def step(k, entered):
            g = c * per_line + k
            rows, s, run, end, v, pushed = push(g, neg_rates_d)
            y = within(rows, s, run, v, skips_d)
            y = y + mm(c_all[rows, :], entered.astype(bf16)) * jnp.exp(run)
            vals[rows, :] = y.astype(bf16)
            return jnp.exp(end) * entered + pushed

        lax.fori_loop(0, per_line, step, jnp.zeros((states, feats), f32))
        return 0

    lax.fori_loop(0, per_peer, line, 0)
    put(send2, mm_tn(to_columns, vals[...]))
    start2, finish2, drain2 = exchange(1, send2, recv2)
    start2()
    drain1()
    finish2()
    z = mm_tn(by_col, take(recv2))
    scale = lax.rsqrt(jnp.mean(z * z, axis=-1, keepdims=True) + 1e-5)
    act = (z * scale * gated[...]).astype(bf16)
    mixed = masked[...].astype(f32) + mm(act, w_out_ref[...])
    out_ref[...] = mixed.astype(bf16).reshape(out_ref.shape)
    drain2()


def on_device(n_rows, n_cols, *args):
    args = [a.reshape(1, -1) if a.ndim == 1 else a for a in args]
    patches = args[0]
    local_rows, width, feats = patches.shape
    tokens = local_rows * width
    heads = args[9].shape[1]
    states = (args[3].shape[1] - heads) // 2
    chunks = local_rows
    piece = (n_rows, local_rows * (width // n_rows), feats)
    big = (tokens, feats)
    vmem = pl.BlockSpec(memory_space=pltpu.VMEM)
    return pl.pallas_call(
        functools.partial(block_kernel, n_rows, n_cols),
        out_shape=jax.ShapeDtypeStruct(patches.shape, bf16),
        in_specs=[vmem] * len(args),
        out_specs=vmem,
        scratch_shapes=[
            pltpu.VMEM(big, bf16),
            pltpu.VMEM(big, bf16),
            pltpu.VMEM((tokens, states), bf16),
            pltpu.VMEM((tokens, states), bf16),
            pltpu.VMEM(big, f32),
            pltpu.VMEM(big, f32),
            pltpu.VMEM(big, f32),
            pltpu.VMEM(big, f32),
            pltpu.VMEM((chunks, states, feats), f32),
            pltpu.VMEM((chunks, 1, feats), f32),
            pltpu.VMEM((chunks, states, feats), bf16),
            pltpu.VMEM((chunks, states, feats), bf16),
            pltpu.VMEM(piece, bf16),
            pltpu.VMEM(piece, bf16),
            pltpu.VMEM(piece, bf16),
            pltpu.VMEM(piece, bf16),
            pltpu.SemaphoreType.DMA((2, n_rows)),
            pltpu.SemaphoreType.DMA((2, n_rows)),
            pltpu.SemaphoreType.DMA((2,)),
        ],
        compiler_params=pltpu.CompilerParams(
            collective_id=0, has_side_effects=True, vmem_limit_bytes=40 * 1024 * 1024
        ),
    )(*args)


def solution(mesh):
    rep = P()
    return jax.shard_map(
        functools.partial(on_device, mesh.shape["rows"], mesh.shape["cols"]),
        mesh=mesh,
        in_specs=(P("rows", "cols", None), P("rows", "cols")) + (rep,) * 13,
        out_specs=P("rows", "cols", None),
        check_vma=False,
    )
```

```python
import functools

import jax
import jax.numpy as jnp
from jax import lax
from jax.experimental import pallas as pl
from jax.experimental.pallas import tpu as pltpu
from jax.sharding import PartitionSpec as P

MESH = pl.DeviceIdType.MESH
f32 = jnp.float32
bf16 = jnp.bfloat16


def mm(a, b):
    return jnp.dot(a, b, preferred_element_type=f32)


def mm_nt(a, b):
    return lax.dot_general(a, b, (((1,), (1,)), ((), ())), preferred_element_type=f32)


def mm_tn(a, b):
    return lax.dot_general(a, b, (((0,), (0,)), ((), ())), preferred_element_type=f32)


def parts_of(x):
    high = x.astype(bf16)
    return high, (x - high.astype(f32)).astype(bf16)


def mm_split_right(a, x):
    high, low = parts_of(x)
    return mm(a, high) + mm(a, low)


def mm_split_left(x, b):
    high, low = parts_of(x)
    return mm(high, b) + mm(low, b)


def iota(shape, dim):
    return lax.broadcasted_iota(jnp.int32, shape, dim)


def log2_of(size):
    assert size & (size - 1) == 0
    return size.bit_length() - 1


def one_hot(index):
    count, lanes = index.shape
    lane = iota(index.shape, 1)
    tiles = [
        jnp.where(index - start == lane, 1.0, 0.0).astype(bf16)
        for start in range(0, count, lanes)
    ]
    return jnp.concatenate(tiles, axis=1)


ARGS = (
    "patches",
    "tissue",
    "w_value",
    "w_across",
    "w_down",
    "w_gate",
    "w_out",
    "bias_a",
    "bias_d",
    "rates_a",
    "rates_d",
    "skip_a",
    "skip_d",
    "gain_a",
    "gain_f",
)
SMALL = ARGS[7:]
LOAD_ORDER = ("tissue", "patches", "w_value", "w_across") + SMALL + ("w_gate", "w_down", "w_out")


def block_kernel(
    n_rows,
    n_cols,
    *refs,
):
    count = len(ARGS)
    sources, out_ref, held = refs[:count], refs[count], refs[count + 1 : 2 * count + 1]
    (
        masked,
        vals,
        b_all,
        c_all,
        bt_all,
        v_all,
        l_exp,
        y_all,
        gated,
        pushed_all,
        l_end,
        state_out,
        state_in,
        send1,
        recv1,
        send2,
        recv2,
        send_sems,
        recv_sems,
        relay_sems,
        load_sems,
    ) = refs[2 * count + 1 :]
    loads = {
        name: pltpu.make_async_copy(sources[k], held[k], load_sems.at[k])
        for k, name in enumerate(ARGS)
    }
    for name in LOAD_ORDER:
        loads[name].start()
    (
        patches_ref,
        tissue_ref,
        w_value_ref,
        w_across_ref,
        w_down_ref,
        w_gate_ref,
        w_out_ref,
        bias_a_ref,
        bias_d_ref,
        rates_a_ref,
        rates_d_ref,
        skip_a_ref,
        skip_d_ref,
        gain_a_ref,
        gain_f_ref,
    ) = held
    local_rows, width, feats = patches_ref.shape
    heads = rates_a_ref.shape[1]
    head_width = feats // heads
    states = (w_across_ref.shape[0] - heads) // 2
    tokens = local_rows * width
    chunk = width
    chunks = tokens // chunk
    per_peer = width // n_rows
    height = n_rows * local_rows
    assert head_width == chunk and height % chunk == 0

    my_row = lax.axis_index("rows")
    my_col = lax.axis_index("cols")

    barrier = pltpu.get_barrier_semaphore()

    @pl.loop(1, n_rows)
    def _(off):
        pl.semaphore_signal(
            barrier,
            inc=1,
            device_id=(lax.rem(my_row + off, n_rows), my_col),
            device_id_type=MESH,
        )

    @pl.when(my_col > 0)
    def _():
        pl.semaphore_signal(
            barrier, inc=1, device_id=(my_row, my_col - 1), device_id_type=MESH
        )

    lane = iota((heads, feats), 1)
    first = iota((heads, feats), 0) * head_width
    expand = jnp.where((lane >= first) & (lane < first + head_width), 1.0, 0.0).astype(bf16)
    place_t = iota((chunk, feats), 0)
    place_u = iota((chunk, feats), 1) & (head_width - 1)
    causal = place_t >= place_u
    diagonal = place_t == place_u
    pair = 2 if chunks % 2 == 0 else 1
    span = pair * chunk
    tri_t, tri_u = iota((span, span), 0), iota((span, span), 1)
    csh = log2_of(chunk)
    tri = jnp.where(
        (tri_t >= tri_u)
        & (lax.shift_right_logical(tri_t, csh) == lax.shift_right_logical(tri_u, csh)),
        1.0,
        0.0,
    ).astype(bf16)
    tri = jnp.concatenate([tri, tri], axis=1)
    group = min(heads, 4)
    gw = group * head_width
    sh = log2_of(head_width)
    same_head = jnp.where(
        lax.shift_right_logical(iota((gw, gw), 0), sh)
        == lax.shift_right_logical(iota((gw, gw), 1), sh),
        1.0,
        0.0,
    ).astype(bf16)

    def wide(ref):
        return mm_split_left(jnp.broadcast_to(ref[...], (8, heads)), expand)[0:1]

    def tall(ref):
        square = jnp.broadcast_to(ref[...], (heads, heads))
        eye = iota((heads, heads), 0) == iota((heads, heads), 1)
        return jnp.sum(jnp.where(eye, square, 0.0), axis=1, keepdims=True)

    def spread(x):
        high, low = parts_of(x)
        return mm_tn(
            jnp.concatenate([high, low], axis=0), jnp.concatenate([expand, expand], axis=0)
        )

    def project(x, w_ref, bias, neg_rates):
        weights = w_ref[...]
        proj = mm_nt(x, weights[: 2 * states])
        b_all[...] = proj[:, :states].astype(bf16)
        c_all[...] = proj[:, states:].astype(bf16)
        turned = mm_nt(weights, x)
        bt_all[...] = turned[:states].astype(bf16)
        v = turned[2 * states :] + bias
        steps = jnp.maximum(v, 0.0) + jnp.log1p(jnp.exp(-jnp.abs(v)))
        v_all[...] = (spread(steps) * vals[...].astype(f32)).astype(bf16)
        high, low = parts_of(spread(steps * neg_rates))
        for g in range(0, chunks, pair):
            rows = slice(g * chunk, (g + pair) * chunk)
            l_exp[rows, :] = mm(tri, jnp.concatenate([high[rows], low[rows]], axis=0))

    def push(g):
        rows = slice(g * chunk, (g + 1) * chunk)
        run = l_exp[rows, :]
        end = run[chunk - 1 : chunk, :]
        scaled = v_all[rows, :].astype(f32) * jnp.exp(end - run)
        return end, mm(bt_all[:, rows], scaled.astype(bf16))

    def within(g, skips):
        rows = slice(g * chunk, (g + 1) * chunk)
        run = l_exp[rows, :]
        run_u = jnp.sum(jnp.where(diagonal, run, 0.0), axis=0, keepdims=True)
        b = b_all[rows, :]
        cb = mm_nt(c_all[rows, :], jnp.concatenate([b] * heads, axis=0))
        decay = jnp.exp(jnp.where(causal, run - run_u, -1e30))
        weights = (decay * cb).astype(bf16)
        vb = v_all[rows, :]
        outs = []
        for q in range(heads // group):
            lanes = slice(q * gw, (q + 1) * gw)
            stacked = jnp.concatenate([vb[:, lanes]] * group, axis=0) * same_head
            outs.append(mm(weights[:, lanes], stacked))
        return jnp.concatenate(outs, axis=1) + skips * vals[rows, :].astype(f32)

    def exchange(slot, source, target):
        def copy_of(off):
            to = lax.rem(my_row + off, n_rows)
            return pltpu.make_async_remote_copy(
                src_ref=source.at[to],
                dst_ref=target.at[my_row],
                send_sem=send_sems.at[slot, off],
                recv_sem=recv_sems.at[slot, off],
                device_id=(to, my_col),
                device_id_type=MESH,
            )

        def start():
            @pl.loop(1, n_rows)
            def _(off):
                copy_of(off).start()

            target[my_row] = source[my_row]

        def finish():
            @pl.loop(1, n_rows)
            def _(off):
                came = lax.rem(my_row + n_rows - off, n_rows)
                pltpu.make_async_remote_copy(
                    src_ref=source.at[came],
                    dst_ref=target.at[came],
                    send_sem=send_sems.at[slot, off],
                    recv_sem=recv_sems.at[slot, off],
                    device_id=(came, my_col),
                    device_id_type=MESH,
                ).wait_recv()

        def drain():
            @pl.loop(1, n_rows)
            def _(off):
                copy_of(off).wait_send()

        return start, finish, drain

    def put(ref, x):
        if ref.shape[1] % 16:
            x = x.astype(f32).reshape(ref.shape).astype(bf16)
        else:
            x = x.astype(bf16).reshape(ref.shape)
        ref[...] = x

    def take(ref):
        x = ref[...]
        if ref.shape[1] % 16:
            return x.astype(f32).reshape(tokens, feats).astype(bf16)
        return x.reshape(tokens, feats)

    rsh = log2_of(local_rows)
    hsh = log2_of(height)
    psh = log2_of(per_peer)
    m = iota((tokens, 128), 0)
    by_col = one_hot(((m & (local_rows - 1)) << csh) + lax.shift_right_logical(m, rsh))
    i_of = m & (height - 1)
    to_columns = one_hot(
        (lax.shift_right_logical(i_of, rsh) << (rsh + psh))
        + (lax.shift_right_logical(m, hsh) << rsh)
        + (i_of & (local_rows - 1))
    )

    loads["tissue"].wait()
    loads["patches"].wait()
    flags = tissue_ref[...].astype(f32).T
    for r in range(local_rows):
        flag = jnp.broadcast_to(flags[:, r : r + 1], (width, feats)) > 0.5
        masked[r * width : (r + 1) * width, :] = jnp.where(
            flag, patches_ref[r].astype(f32), 0.0
        ).astype(bf16)

    for name in ("w_value", "w_across") + SMALL:
        loads[name].wait()
    x = masked[...]
    vals[...] = mm(x, w_value_ref[...]).astype(bf16)
    project(x, w_across_ref, tall(bias_a_ref), -tall(rates_a_ref))
    skips = wide(skip_a_ref)

    for g in range(chunks):
        l_end[g], pushed_all[g] = push(g)

    greeted = n_rows - 1 + jnp.where(my_col < n_cols - 1, 1, 0)
    pl.semaphore_wait(barrier, greeted)

    relay = pltpu.make_async_remote_copy(
        src_ref=state_out,
        dst_ref=state_in,
        send_sem=relay_sems.at[0],
        recv_sem=relay_sems.at[1],
        device_id=(my_row, lax.rem(my_col + 1, n_cols)),
        device_id_type=MESH,
    )

    @pl.when(my_col == 0)
    def _():
        state_in[...] = jnp.zeros_like(state_in)
        if n_cols > 1:
            state_out[...] = pushed_all[...].astype(bf16)
            relay.start()

    for g in range(chunks):
        y_all[g * chunk : (g + 1) * chunk, :] = within(g, skips)

    @pl.when(my_col > 0)
    def _():
        relay.wait_recv()

        @pl.when(my_col < n_cols - 1)
        def _():
            state_out[...] = (
                pushed_all[...] + jnp.exp(l_end[...]) * state_in[...].astype(f32)
            ).astype(bf16)
            relay.start()

    gain_a = gain_a_ref[...]
    for g in range(chunks):
        rows = slice(g * chunk, (g + 1) * chunk)
        y = y_all[rows, :] + mm(c_all[rows, :], state_in[g]) * jnp.exp(l_exp[rows, :])
        scale = lax.rsqrt(jnp.mean(y * y, axis=-1, keepdims=True) + 1e-5)
        vals[rows, :] = (y * scale * gain_a).astype(bf16)

    put(send1, mm(by_col, vals[...]))
    start1, finish1, drain1 = exchange(0, send1, recv1)
    start1()

    loads["w_gate"].wait()
    gate = mm(masked[...], w_gate_ref[...])
    gated[...] = gate / (1.0 + jnp.exp(-gate)) * gain_f_ref[...]
    skips_d = wide(skip_d_ref)
    bias_d, neg_rates_d = tall(bias_d_ref), -tall(rates_d_ref)
    loads["w_down"].wait()
    loads["w_out"].wait()

    @pl.when(my_col < n_cols - 1)
    def _():
        relay.wait_send()

    finish1()
    cols = mm(to_columns, take(recv1)).astype(bf16)
    vals[...] = cols
    project(cols, w_down_ref, bias_d, neg_rates_d)

    per_line = height // chunk
    for c in range(per_peer):
        entered = None
        for g in range(c * per_line, (c + 1) * per_line):
            rows = slice(g * chunk, (g + 1) * chunk)
            end, pushed = push(g)
            y = within(g, skips_d)
            if entered is None:
                entered = pushed
            else:
                y = y + mm(c_all[rows, :], entered.astype(bf16)) * jnp.exp(l_exp[rows, :])
                entered = jnp.exp(end) * entered + pushed
            y_all[rows, :] = y

    put(send2, mm_tn(to_columns, y_all[...].astype(bf16)))
    start2, finish2, drain2 = exchange(1, send2, recv2)
    start2()
    drain1()
    finish2()
    z = mm_tn(by_col, take(recv2))
    scale = lax.rsqrt(jnp.mean(z * z, axis=-1, keepdims=True) + 1e-5)
    act = (z * scale * gated[...]).astype(bf16)
    mixed = masked[...].astype(f32) + mm(act, w_out_ref[...])
    out_ref[...] = mixed.astype(bf16).reshape(out_ref.shape)
    drain2()


def on_device(n_rows, n_cols, *args):
    args = [a.reshape(1, -1) if a.ndim == 1 else a for a in args]
    args[3], args[4] = args[3].T, args[4].T
    patches = args[0]
    local_rows, width, feats = patches.shape
    tokens = local_rows * width
    heads = args[9].shape[1]
    states = (args[3].shape[0] - heads) // 2
    chunks = local_rows
    piece = (n_rows, local_rows * (width // n_rows), feats)
    big = (tokens, feats)
    vmem = pl.BlockSpec(memory_space=pltpu.VMEM)
    return pl.pallas_call(
        functools.partial(block_kernel, n_rows, n_cols),
        out_shape=jax.ShapeDtypeStruct(patches.shape, bf16),
        in_specs=[pl.BlockSpec(memory_space=pl.ANY)] * len(args),
        out_specs=vmem,
        scratch_shapes=[pltpu.VMEM(a.shape, a.dtype) for a in args]
        + [
            pltpu.VMEM(big, bf16),
            pltpu.VMEM(big, bf16),
            pltpu.VMEM((tokens, states), bf16),
            pltpu.VMEM((tokens, states), bf16),
            pltpu.VMEM((states, tokens), bf16),
            pltpu.VMEM(big, bf16),
            pltpu.VMEM(big, f32),
            pltpu.VMEM(big, f32),
            pltpu.VMEM(big, f32),
            pltpu.VMEM((chunks, states, feats), f32),
            pltpu.VMEM((chunks, 1, feats), f32),
            pltpu.VMEM((chunks, states, feats), bf16),
            pltpu.VMEM((chunks, states, feats), bf16),
            pltpu.VMEM(piece, bf16),
            pltpu.VMEM(piece, bf16),
            pltpu.VMEM(piece, bf16),
            pltpu.VMEM(piece, bf16),
            pltpu.SemaphoreType.DMA((2, n_rows)),
            pltpu.SemaphoreType.DMA((2, n_rows)),
            pltpu.SemaphoreType.DMA((2,)),
            pltpu.SemaphoreType.DMA((len(args),)),
        ],
        compiler_params=pltpu.CompilerParams(
            collective_id=0, has_side_effects=True, vmem_limit_bytes=56 * 1024 * 1024
        ),
    )(*args)


def solution(mesh):
    rep = P()
    return jax.shard_map(
        functools.partial(on_device, mesh.shape["rows"], mesh.shape["cols"]),
        mesh=mesh,
        in_specs=(P("rows", "cols", None), P("rows", "cols")) + (rep,) * 13,
        out_specs=P("rows", "cols", None),
        check_vma=False,
    )
```

```python
import functools

import jax
import jax.numpy as jnp
from jax import lax
from jax.experimental import pallas as pl
from jax.experimental.pallas import tpu as pltpu
from jax.sharding import PartitionSpec as P

MESH = pl.DeviceIdType.MESH
GROUPS = 2
STAGES = 2
f32 = jnp.float32
bf16 = jnp.bfloat16


def mm(a, b):
    return jnp.dot(a, b, preferred_element_type=f32)


def mm_nt(a, b):
    return lax.dot_general(a, b, (((1,), (1,)), ((), ())), preferred_element_type=f32)


def mm_tn(a, b):
    return lax.dot_general(a, b, (((0,), (0,)), ((), ())), preferred_element_type=f32)


def parts_of(x):
    high = x.astype(bf16)
    return high, (x - high.astype(f32)).astype(bf16)


def mm_split_right(a, x):
    high, low = parts_of(x)
    return mm(a, high) + mm(a, low)


def mm_split_left(x, b):
    high, low = parts_of(x)
    return mm(high, b) + mm(low, b)


def iota(shape, dim):
    return lax.broadcasted_iota(jnp.int32, shape, dim)


def log2_of(size):
    assert size & (size - 1) == 0
    return size.bit_length() - 1


def one_hot(index):
    count, lanes = index.shape
    lane = iota(index.shape, 1)
    tiles = [
        jnp.where(index - start == lane, 1.0, 0.0).astype(bf16)
        for start in range(0, count, lanes)
    ]
    return jnp.concatenate(tiles, axis=1)


ARGS = (
    "patches",
    "tissue",
    "w_value",
    "w_across",
    "w_down",
    "w_gate",
    "w_out",
    "bias_a",
    "bias_d",
    "rates_a",
    "rates_d",
    "skip_a",
    "skip_d",
    "gain_a",
    "gain_f",
)
SMALL = ARGS[7:]
LOAD_ORDER = ("tissue", "patches", "w_value", "w_across") + SMALL + ("w_gate", "w_down", "w_out")


def block_kernel(
    n_rows,
    n_cols,
    *refs,
):
    count = len(ARGS)
    sources, out_ref, held = refs[:count], refs[count], refs[count + 1 : 2 * count + 1]
    (
        masked,
        vals,
        b_all,
        c_all,
        bt_all,
        v_all,
        l_exp,
        y_all,
        gated,
        pushed_all,
        l_end,
        state_out,
        state_in,
        send1,
        recv1,
        send2,
        recv2,
        send_sems,
        recv_sems,
        relay_sems,
        down_out,
        down_in,
        down_sems,
        load_sems,
    ) = refs[2 * count + 1 :]
    loads = {
        name: pltpu.make_async_copy(sources[k], held[k], load_sems.at[k])
        for k, name in enumerate(ARGS)
    }
    for name in LOAD_ORDER:
        loads[name].start()
    (
        patches_ref,
        tissue_ref,
        w_value_ref,
        w_across_ref,
        w_down_ref,
        w_gate_ref,
        w_out_ref,
        bias_a_ref,
        bias_d_ref,
        rates_a_ref,
        rates_d_ref,
        skip_a_ref,
        skip_d_ref,
        gain_a_ref,
        gain_f_ref,
    ) = held
    local_rows, width, feats = patches_ref.shape
    heads = rates_a_ref.shape[1]
    head_width = feats // heads
    states = (w_across_ref.shape[0] - heads) // 2
    tokens = local_rows * width
    chunk = width
    chunks = tokens // chunk
    members = n_rows // GROUPS
    per_peer = width // members
    height = members * local_rows
    stage_tokens = tokens // STAGES
    stage_chunks = chunks // STAGES
    stage_lines = per_peer // STAGES
    per_line = height // chunk
    assert head_width == chunk and height % chunk == 0

    my_row = lax.axis_index("rows")
    my_col = lax.axis_index("cols")

    barrier = pltpu.get_barrier_semaphore()

    group_of = my_row // members
    member = lax.rem(my_row, members)
    base = group_of * members

    def fellow(off):
        return lax.rem(member + off, members)

    @pl.loop(1, members)
    def _(off):
        pl.semaphore_signal(
            barrier, inc=1, device_id=(base + fellow(off), my_col), device_id_type=MESH
        )

    @pl.when(group_of > 0)
    def _():
        pl.semaphore_signal(
            barrier, inc=1, device_id=(my_row - members, my_col), device_id_type=MESH
        )

    @pl.when(my_col > 0)
    def _():
        pl.semaphore_signal(
            barrier, inc=1, device_id=(my_row, my_col - 1), device_id_type=MESH
        )

    lane = iota((heads, feats), 1)
    first = iota((heads, feats), 0) * head_width
    expand = jnp.where((lane >= first) & (lane < first + head_width), 1.0, 0.0).astype(bf16)
    place_t = iota((chunk, feats), 0)
    place_u = iota((chunk, feats), 1) & (head_width - 1)
    causal = place_t >= place_u
    diagonal = place_t == place_u
    pair = 2 if stage_chunks % 2 == 0 else 1
    span = pair * chunk
    tri_t, tri_u = iota((span, span), 0), iota((span, span), 1)
    csh = log2_of(chunk)
    tri = jnp.where(
        (tri_t >= tri_u)
        & (lax.shift_right_logical(tri_t, csh) == lax.shift_right_logical(tri_u, csh)),
        1.0,
        0.0,
    ).astype(bf16)
    tri = jnp.concatenate([tri, tri], axis=1)
    group = min(heads, 4)
    gw = group * head_width
    sh = log2_of(head_width)
    same_head = jnp.where(
        lax.shift_right_logical(iota((gw, gw), 0), sh)
        == lax.shift_right_logical(iota((gw, gw), 1), sh),
        1.0,
        0.0,
    ).astype(bf16)

    def wide(ref):
        return mm_split_left(jnp.broadcast_to(ref[...], (8, heads)), expand)[0:1]

    def tall(ref):
        square = jnp.broadcast_to(ref[...], (heads, heads))
        eye = iota((heads, heads), 0) == iota((heads, heads), 1)
        return jnp.sum(jnp.where(eye, square, 0.0), axis=1, keepdims=True)

    def spread(x):
        high, low = parts_of(x)
        return mm_tn(
            jnp.concatenate([high, low], axis=0), jnp.concatenate([expand, expand], axis=0)
        )

    def project(x, w_ref, bias, neg_rates, start=0):
        here = slice(start, start + x.shape[0])
        weights = w_ref[...]
        proj = mm_nt(x, weights[: 2 * states])
        b_all[here, :] = proj[:, :states].astype(bf16)
        c_all[here, :] = proj[:, states:].astype(bf16)
        turned = mm_nt(weights, x)
        bt_all[:, here] = turned[:states].astype(bf16)
        v = turned[2 * states :] + bias
        steps = jnp.maximum(v, 0.0) + jnp.log1p(jnp.exp(-jnp.abs(v)))
        v_all[here, :] = (spread(steps) * vals[here, :].astype(f32)).astype(bf16)
        high, low = parts_of(spread(steps * neg_rates))
        for g in range(0, x.shape[0], span):
            rows = slice(g, g + span)
            l_exp[start + g : start + g + span, :] = mm(tri, jnp.concatenate([high[rows], low[rows]], axis=0))

    def push(g):
        rows = slice(g * chunk, (g + 1) * chunk)
        run = l_exp[rows, :]
        end = run[chunk - 1 : chunk, :]
        scaled = v_all[rows, :].astype(f32) * jnp.exp(end - run)
        return end, mm(bt_all[:, rows], scaled.astype(bf16))

    def within(g, skips):
        rows = slice(g * chunk, (g + 1) * chunk)
        run = l_exp[rows, :]
        run_u = jnp.sum(jnp.where(diagonal, run, 0.0), axis=0, keepdims=True)
        b = b_all[rows, :]
        cb = mm_nt(c_all[rows, :], jnp.concatenate([b] * heads, axis=0))
        decay = jnp.exp(jnp.where(causal, run - run_u, -1e30))
        weights = (decay * cb).astype(bf16)
        vb = v_all[rows, :]
        outs = []
        for q in range(heads // group):
            lanes = slice(q * gw, (q + 1) * gw)
            stacked = jnp.concatenate([vb[:, lanes]] * group, axis=0) * same_head
            outs.append(mm(weights[:, lanes], stacked))
        return jnp.concatenate(outs, axis=1) + skips * vals[rows, :].astype(f32)

    def exchange(slot, stage, source, target):
        source, target = source.at[stage], target.at[stage]

        def copy_of(off, to, place):
            return pltpu.make_async_remote_copy(
                src_ref=source.at[to],
                dst_ref=target.at[place],
                send_sem=send_sems.at[slot, stage, off],
                recv_sem=recv_sems.at[slot, stage, off],
                device_id=(base + to, my_col),
                device_id_type=MESH,
            )

        def start():
            @pl.loop(1, members)
            def _(off):
                copy_of(off, fellow(off), member).start()

            target[member] = source[member]

        def finish():
            @pl.loop(1, members)
            def _(off):
                came = fellow(members - off)
                copy_of(off, came, came).wait_recv()

        def drain():
            @pl.loop(1, members)
            def _(off):
                copy_of(off, fellow(off), member).wait_send()

        return start, finish, drain

    def put(ref, x):
        if ref.shape[-2] % 16:
            x = x.astype(f32).reshape(ref.shape).astype(bf16)
        else:
            x = x.astype(bf16).reshape(ref.shape)
        ref[...] = x

    def take(ref):
        x = ref[...]
        if ref.shape[-2] % 16:
            return x.astype(f32).reshape(-1, feats).astype(bf16)
        return x.reshape(-1, feats)

    rsh = log2_of(local_rows)
    hsh = log2_of(height)
    lsh = log2_of(stage_lines)
    msh = log2_of(members)
    m = iota((tokens, 128), 0)
    shr = lax.shift_right_logical
    by_col = one_hot(
        ((m & (local_rows - 1)) << csh)
        + ((shr(m, rsh + lsh) & (members - 1)) << log2_of(per_peer))
        + (shr(m, rsh + lsh + msh) << lsh)
        + (shr(m, rsh) & (stage_lines - 1))
    )
    m = iota((stage_tokens, 128), 0)
    i_of = m & (height - 1)
    to_columns = one_hot(
        (shr(i_of, rsh) << (rsh + lsh)) + (shr(m, hsh) << rsh) + (i_of & (local_rows - 1))
    )

    loads["tissue"].wait()
    loads["patches"].wait()
    flags = tissue_ref[...].astype(f32).T
    for r in range(local_rows):
        flag = jnp.broadcast_to(flags[:, r : r + 1], (width, feats)) > 0.5
        masked[r * width : (r + 1) * width, :] = jnp.where(
            flag, patches_ref[r].astype(f32), 0.0
        ).astype(bf16)

    for name in ("w_value", "w_across") + SMALL:
        loads[name].wait()
    x = masked[...]
    vals[...] = mm(x, w_value_ref[...]).astype(bf16)
    project(x, w_across_ref, tall(bias_a_ref), -tall(rates_a_ref))
    skips = wide(skip_a_ref)

    for g in range(chunks):
        l_end[g], pushed_all[g] = push(g)

    greeted = (
        members
        - 1
        + jnp.where(my_col < n_cols - 1, 1, 0)
        + jnp.where(group_of < GROUPS - 1, 1, 0)
    )
    pl.semaphore_wait(barrier, greeted)

    relay = pltpu.make_async_remote_copy(
        src_ref=state_out,
        dst_ref=state_in,
        send_sem=relay_sems.at[0],
        recv_sem=relay_sems.at[1],
        device_id=(my_row, lax.rem(my_col + 1, n_cols)),
        device_id_type=MESH,
    )

    @pl.when(my_col == 0)
    def _():
        state_in[...] = jnp.zeros_like(state_in)
        if n_cols > 1:
            state_out[...] = pushed_all[...].astype(bf16)
            relay.start()

    for g in range(chunks):
        y_all[g * chunk : (g + 1) * chunk, :] = within(g, skips)

    @pl.when(my_col > 0)
    def _():
        relay.wait_recv()

        @pl.when(my_col < n_cols - 1)
        def _():
            state_out[...] = (
                pushed_all[...] + jnp.exp(l_end[...]) * state_in[...].astype(f32)
            ).astype(bf16)
            relay.start()

    gain_a = gain_a_ref[...]
    for g in range(chunks):
        rows = slice(g * chunk, (g + 1) * chunk)
        y = y_all[rows, :] + mm(c_all[rows, :], state_in[g]) * jnp.exp(l_exp[rows, :])
        scale = lax.rsqrt(jnp.mean(y * y, axis=-1, keepdims=True) + 1e-5)
        vals[rows, :] = (y * scale * gain_a).astype(bf16)

    put(send1, mm(by_col, vals[...]))
    across = [exchange(0, k, send1, recv1) for k in range(STAGES)]
    for start, _, _ in across:
        start()

    loads["w_gate"].wait()
    gate = mm(masked[...], w_gate_ref[...])
    gated[...] = gate / (1.0 + jnp.exp(-gate)) * gain_f_ref[...]
    skips_d = wide(skip_d_ref)
    bias_d, neg_rates_d = tall(bias_d_ref), -tall(rates_d_ref)
    loads["w_down"].wait()
    loads["w_out"].wait()

    @pl.when(my_col < n_cols - 1)
    def _():
        relay.wait_send()

    hand_down = [
        pltpu.make_async_remote_copy(
            src_ref=down_out.at[k],
            dst_ref=down_in.at[k],
            send_sem=down_sems.at[0, k],
            recv_sem=down_sems.at[1, k],
            device_id=(lax.rem(my_row + members, n_rows), my_col),
            device_id_type=MESH,
        )
        for k in range(STAGES)
    ]

    @pl.when(group_of == 0)
    def _():
        down_in[...] = jnp.zeros_like(down_in)

    for k in range(STAGES):
        across[k][1]()
        first_token = k * stage_tokens
        cols = mm(to_columns, take(recv1.at[k])).astype(bf16)
        vals[first_token : first_token + stage_tokens, :] = cols
        project(cols, w_down_ref, bias_d, neg_rates_d, first_token)
        for c in range(stage_lines):
            entered = None
            for i in range(per_line):
                g = k * stage_chunks + c * per_line + i
                end, pushed = push(g)
                l_end[g], pushed_all[g] = end, pushed
                entered = pushed if entered is None else jnp.exp(end) * entered + pushed
            down_out[k, c] = entered.astype(bf16)

        @pl.when(group_of < GROUPS - 1)
        def _():
            hand_down[k].start()

    back = [exchange(1, k, send2, recv2) for k in range(STAGES)]
    for k in range(STAGES):
        for g in range(k * stage_chunks, (k + 1) * stage_chunks):
            y_all[g * chunk : (g + 1) * chunk, :] = within(g, skips_d)

        @pl.when(group_of > 0)
        def _():
            hand_down[k].wait_recv()

        parts = []
        for c in range(stage_lines):
            entered = down_in[k, c].astype(f32)
            for i in range(per_line):
                g = k * stage_chunks + c * per_line + i
                rows = slice(g * chunk, (g + 1) * chunk)
                extra = mm(c_all[rows, :], entered.astype(bf16)) * jnp.exp(l_exp[rows, :])
                parts.append((y_all[rows, :] + extra).astype(bf16))
                if i < per_line - 1:
                    entered = jnp.exp(l_end[g]) * entered + pushed_all[g]
        put(send2.at[k], mm_tn(to_columns, jnp.concatenate(parts, axis=0)))
        back[k][0]()

    for _, _, drain in across:
        drain()

    @pl.when(group_of < GROUPS - 1)
    def _():
        for copy in hand_down:
            copy.wait_send()

    for _, finish, _ in back:
        finish()
    z = mm_tn(by_col, take(recv2))
    scale = lax.rsqrt(jnp.mean(z * z, axis=-1, keepdims=True) + 1e-5)
    act = (z * scale * gated[...]).astype(bf16)
    mixed = masked[...].astype(f32) + mm(act, w_out_ref[...])
    out_ref[...] = mixed.astype(bf16).reshape(out_ref.shape)
    for _, _, drain in back:
        drain()


def on_device(n_rows, n_cols, *args):
    args = [a.reshape(1, -1) if a.ndim == 1 else a for a in args]
    args[3], args[4] = args[3].T, args[4].T
    patches = args[0]
    local_rows, width, feats = patches.shape
    tokens = local_rows * width
    heads = args[9].shape[1]
    states = (args[3].shape[0] - heads) // 2
    chunks = local_rows
    members = n_rows // GROUPS
    stage_lines = width // members // STAGES
    piece = (STAGES, members, local_rows * stage_lines, feats)
    down = (STAGES, stage_lines, states, feats)
    big = (tokens, feats)
    vmem = pl.BlockSpec(memory_space=pltpu.VMEM)
    return pl.pallas_call(
        functools.partial(block_kernel, n_rows, n_cols),
        out_shape=jax.ShapeDtypeStruct(patches.shape, bf16),
        in_specs=[pl.BlockSpec(memory_space=pl.ANY)] * len(args),
        out_specs=vmem,
        scratch_shapes=[pltpu.VMEM(a.shape, a.dtype) for a in args]
        + [
            pltpu.VMEM(big, bf16),
            pltpu.VMEM(big, bf16),
            pltpu.VMEM((tokens, states), bf16),
            pltpu.VMEM((tokens, states), bf16),
            pltpu.VMEM((states, tokens), bf16),
            pltpu.VMEM(big, bf16),
            pltpu.VMEM(big, f32),
            pltpu.VMEM(big, f32),
            pltpu.VMEM(big, f32),
            pltpu.VMEM((chunks, states, feats), f32),
            pltpu.VMEM((chunks, 1, feats), f32),
            pltpu.VMEM((chunks, states, feats), bf16),
            pltpu.VMEM((chunks, states, feats), bf16),
            pltpu.VMEM(piece, bf16),
            pltpu.VMEM(piece, bf16),
            pltpu.VMEM(piece, bf16),
            pltpu.VMEM(piece, bf16),
            pltpu.SemaphoreType.DMA((2, STAGES, members)),
            pltpu.SemaphoreType.DMA((2, STAGES, members)),
            pltpu.SemaphoreType.DMA((2,)),
            pltpu.VMEM(down, bf16),
            pltpu.VMEM(down, bf16),
            pltpu.SemaphoreType.DMA((2, STAGES)),
            pltpu.SemaphoreType.DMA((len(args),)),
        ],
        compiler_params=pltpu.CompilerParams(
            collective_id=0, has_side_effects=True, vmem_limit_bytes=56 * 1024 * 1024
        ),
    )(*args)


def solution(mesh):
    rep = P()
    return jax.shard_map(
        functools.partial(on_device, mesh.shape["rows"], mesh.shape["cols"]),
        mesh=mesh,
        in_specs=(P("rows", "cols", None), P("rows", "cols")) + (rep,) * 13,
        out_specs=P("rows", "cols", None),
        check_vma=False,
    )
```

```python
import functools

import jax
import jax.numpy as jnp
from jax import lax
from jax.experimental import pallas as pl
from jax.experimental.pallas import tpu as pltpu
from jax.sharding import PartitionSpec as P

MESH = pl.DeviceIdType.MESH
GROUPS = 2
STAGES = 2
HALVES = 2
f32 = jnp.float32
bf16 = jnp.bfloat16


def mm(a, b):
    return jnp.dot(a, b, preferred_element_type=f32)


def mm_nt(a, b):
    return lax.dot_general(a, b, (((1,), (1,)), ((), ())), preferred_element_type=f32)


def mm_tn(a, b):
    return lax.dot_general(a, b, (((0,), (0,)), ((), ())), preferred_element_type=f32)


def parts_of(x):
    high = x.astype(bf16)
    return high, (x - high.astype(f32)).astype(bf16)


def mm_split_right(a, x):
    high, low = parts_of(x)
    return mm(a, high) + mm(a, low)


def mm_split_left(x, b):
    high, low = parts_of(x)
    return mm(high, b) + mm(low, b)


def iota(shape, dim):
    return lax.broadcasted_iota(jnp.int32, shape, dim)


def log2_of(size):
    assert size & (size - 1) == 0
    return size.bit_length() - 1


def one_hot(index):
    count, lanes = index.shape
    lane = iota(index.shape, 1)
    tiles = [
        jnp.where(index - start == lane, 1.0, 0.0).astype(bf16)
        for start in range(0, count, lanes)
    ]
    return jnp.concatenate(tiles, axis=1)


ARGS = (
    "patches",
    "tissue",
    "w_value",
    "w_across",
    "w_down",
    "w_gate",
    "w_out",
    "bias_a",
    "bias_d",
    "rates_a",
    "rates_d",
    "skip_a",
    "skip_d",
    "gain_a",
    "gain_f",
)
SMALL = ARGS[7:]
LOAD_ORDER = ("tissue", "patches", "w_value", "w_across") + SMALL + ("w_gate", "w_down", "w_out")


def block_kernel(
    n_rows,
    n_cols,
    *refs,
):
    count = len(ARGS)
    sources, out_ref, held = refs[:count], refs[count], refs[count + 1 : 2 * count + 1]
    (
        masked,
        vals,
        b_all,
        c_all,
        bt_all,
        v_all,
        l_exp,
        y_all,
        gated,
        ordered,
        mixed_all,
        pushed_all,
        l_end,
        state_out,
        state_in,
        send1,
        recv1,
        send2,
        recv2,
        send_sems,
        recv_sems,
        relay_sems,
        down_out,
        down_in,
        down_sems,
        load_sems,
    ) = refs[2 * count + 1 :]
    loads = {
        name: pltpu.make_async_copy(sources[k], held[k], load_sems.at[k])
        for k, name in enumerate(ARGS)
    }
    for name in LOAD_ORDER:
        loads[name].start()
    (
        patches_ref,
        tissue_ref,
        w_value_ref,
        w_across_ref,
        w_down_ref,
        w_gate_ref,
        w_out_ref,
        bias_a_ref,
        bias_d_ref,
        rates_a_ref,
        rates_d_ref,
        skip_a_ref,
        skip_d_ref,
        gain_a_ref,
        gain_f_ref,
    ) = held
    local_rows, width, feats = patches_ref.shape
    heads = rates_a_ref.shape[1]
    head_width = feats // heads
    states = (w_across_ref.shape[0] - heads) // 2
    tokens = local_rows * width
    chunk = width
    chunks = tokens // chunk
    members = n_rows // GROUPS
    per_peer = width // members
    height = members * local_rows
    stage_tokens = tokens // STAGES
    stage_chunks = chunks // STAGES
    half_rows = local_rows // HALVES
    half_tokens = tokens // HALVES
    stage_lines = per_peer // STAGES
    per_line = height // chunk
    assert head_width == chunk and height % chunk == 0

    my_row = lax.axis_index("rows")
    my_col = lax.axis_index("cols")

    barrier = pltpu.get_barrier_semaphore()

    group_of = my_row // members
    member = lax.rem(my_row, members)
    base = group_of * members

    def fellow(off):
        return lax.rem(member + off, members)

    @pl.loop(1, members)
    def _(off):
        pl.semaphore_signal(
            barrier, inc=1, device_id=(base + fellow(off), my_col), device_id_type=MESH
        )

    @pl.when(group_of > 0)
    def _():
        pl.semaphore_signal(
            barrier, inc=1, device_id=(my_row - members, my_col), device_id_type=MESH
        )

    @pl.when(my_col > 0)
    def _():
        pl.semaphore_signal(
            barrier, inc=1, device_id=(my_row, my_col - 1), device_id_type=MESH
        )

    lane = iota((heads, feats), 1)
    first = iota((heads, feats), 0) * head_width
    expand = jnp.where((lane >= first) & (lane < first + head_width), 1.0, 0.0).astype(bf16)
    place_t = iota((chunk, feats), 0)
    place_u = iota((chunk, feats), 1) & (head_width - 1)
    causal = place_t >= place_u
    diagonal = place_t == place_u
    pair = 2 if stage_chunks % 2 == 0 else 1
    span = pair * chunk
    tri_t, tri_u = iota((span, span), 0), iota((span, span), 1)
    csh = log2_of(chunk)
    tri = jnp.where(
        (tri_t >= tri_u)
        & (lax.shift_right_logical(tri_t, csh) == lax.shift_right_logical(tri_u, csh)),
        1.0,
        0.0,
    ).astype(bf16)
    tri = jnp.concatenate([tri, tri], axis=1)
    group = min(heads, 4)
    gw = group * head_width
    sh = log2_of(head_width)
    same_head = jnp.where(
        lax.shift_right_logical(iota((gw, gw), 0), sh)
        == lax.shift_right_logical(iota((gw, gw), 1), sh),
        1.0,
        0.0,
    ).astype(bf16)

    def wide(ref):
        return mm_split_left(jnp.broadcast_to(ref[...], (8, heads)), expand)[0:1]

    def tall(ref):
        square = jnp.broadcast_to(ref[...], (heads, heads))
        eye = iota((heads, heads), 0) == iota((heads, heads), 1)
        return jnp.sum(jnp.where(eye, square, 0.0), axis=1, keepdims=True)

    def spread(x):
        high, low = parts_of(x)
        return mm_tn(
            jnp.concatenate([high, low], axis=0), jnp.concatenate([expand, expand], axis=0)
        )

    def project(x, w_ref, bias, neg_rates, start=0):
        here = slice(start, start + x.shape[0])
        weights = w_ref[...]
        proj = mm_nt(x, weights[: 2 * states])
        b_all[here, :] = proj[:, :states].astype(bf16)
        c_all[here, :] = proj[:, states:].astype(bf16)
        turned = mm_nt(weights, x)
        bt_all[:, here] = turned[:states].astype(bf16)
        v = turned[2 * states :] + bias
        steps = jnp.maximum(v, 0.0) + jnp.log1p(jnp.exp(-jnp.abs(v)))
        v_all[here, :] = (spread(steps) * vals[here, :].astype(f32)).astype(bf16)
        high, low = parts_of(spread(steps * neg_rates))
        for g in range(0, x.shape[0], span):
            rows = slice(g, g + span)
            l_exp[start + g : start + g + span, :] = mm(tri, jnp.concatenate([high[rows], low[rows]], axis=0))

    def push(g):
        rows = slice(g * chunk, (g + 1) * chunk)
        run = l_exp[rows, :]
        end = run[chunk - 1 : chunk, :]
        scaled = v_all[rows, :].astype(f32) * jnp.exp(end - run)
        return end, mm(bt_all[:, rows], scaled.astype(bf16))

    def within(g, skips):
        rows = slice(g * chunk, (g + 1) * chunk)
        run = l_exp[rows, :]
        run_u = jnp.sum(jnp.where(diagonal, run, 0.0), axis=0, keepdims=True)
        b = b_all[rows, :]
        cb = mm_nt(c_all[rows, :], jnp.concatenate([b] * heads, axis=0))
        decay = jnp.exp(jnp.where(causal, run - run_u, -1e30))
        weights = (decay * cb).astype(bf16)
        vb = v_all[rows, :]
        outs = []
        for q in range(heads // group):
            lanes = slice(q * gw, (q + 1) * gw)
            stacked = jnp.concatenate([vb[:, lanes]] * group, axis=0) * same_head
            outs.append(mm(weights[:, lanes], stacked))
        return jnp.concatenate(outs, axis=1) + skips * vals[rows, :].astype(f32)

    def exchange(source, target, sems, part):
        def copy_of(off, to, place):
            return pltpu.make_async_remote_copy(
                src_ref=source.at[(to,) + part],
                dst_ref=target.at[(place,) + part],
                send_sem=send_sems.at[sems, off],
                recv_sem=recv_sems.at[sems, off],
                device_id=(base + to, my_col),
                device_id_type=MESH,
            )

        def start():
            @pl.loop(1, members)
            def _(off):
                copy_of(off, fellow(off), member).start()

            target[(member,) + part] = source[(member,) + part]

        def finish():
            @pl.loop(1, members)
            def _(off):
                came = fellow(members - off)
                copy_of(off, came, came).wait_recv()

        def drain():
            @pl.loop(1, members)
            def _(off):
                copy_of(off, fellow(off), member).wait_send()

        return start, finish, drain

    def shaped(x, shape):
        if shape[-2] % 16:
            return x.astype(f32).reshape(shape).astype(bf16)
        return x.astype(bf16).reshape(shape)

    def flat(x):
        if x.shape[-2] % 16:
            return x.astype(f32).reshape(-1, feats).astype(bf16)
        return x.reshape(-1, feats)

    rsh = log2_of(half_rows)
    hsh = log2_of(height)
    lsh = log2_of(stage_lines)
    msh = log2_of(members)
    shr = lax.shift_right_logical
    m = iota((half_tokens, 128), 0)
    by_col = one_hot(
        ((m & (half_rows - 1)) << csh)
        + ((shr(m, rsh + lsh) & (members - 1)) << log2_of(per_peer))
        + (shr(m, rsh + lsh + msh) << lsh)
        + (shr(m, rsh) & (stage_lines - 1))
    )
    m = iota((stage_tokens, 128), 0)
    i_of = m & (height - 1)
    to_columns = one_hot(
        (shr(i_of, rsh) << (rsh + lsh)) + (shr(m, hsh) << rsh) + (i_of & (half_rows - 1))
    )

    def half(h):
        return slice(h * half_tokens, (h + 1) * half_tokens)

    def out_order(ref, h, x):
        x = mm(by_col, x)
        ref[:, :, h] = shaped(x, (STAGES, members) + ref.shape[3:])

    loads["tissue"].wait()
    loads["patches"].wait()
    flags = tissue_ref[...].astype(f32).T
    for r in range(local_rows):
        flag = jnp.broadcast_to(flags[:, r : r + 1], (width, feats)) > 0.5
        masked[r * width : (r + 1) * width, :] = jnp.where(
            flag, patches_ref[r].astype(f32), 0.0
        ).astype(bf16)

    for name in ("w_value", "w_across") + SMALL:
        loads[name].wait()
    x = masked[...]
    vals[...] = mm(x, w_value_ref[...]).astype(bf16)
    project(x, w_across_ref, tall(bias_a_ref), -tall(rates_a_ref))
    skips = wide(skip_a_ref)

    relays = [
        pltpu.make_async_remote_copy(
            src_ref=state_out.at[pl.ds(h * half_rows, half_rows)],
            dst_ref=state_in.at[pl.ds(h * half_rows, half_rows)],
            send_sem=relay_sems.at[0, h],
            recv_sem=relay_sems.at[1, h],
            device_id=(my_row, lax.rem(my_col + 1, n_cols)),
            device_id_type=MESH,
        )
        for h in range(HALVES)
    ]

    def rows_of(h):
        return range(h * half_rows, (h + 1) * half_rows)

    @pl.when(my_col < n_cols - 1)
    def _():
        for g in range(chunks):
            l_end[g], pushed_all[g] = push(g)

    greeted = (
        members
        - 1
        + jnp.where(my_col < n_cols - 1, 1, 0)
        + jnp.where(group_of < GROUPS - 1, 1, 0)
    )
    pl.semaphore_wait(barrier, greeted)

    @pl.when(my_col == 0)
    def _():
        state_in[...] = jnp.zeros_like(state_in)
        if n_cols > 1:
            for h in range(HALVES):
                for g in rows_of(h):
                    state_out[g] = pushed_all[g].astype(bf16)
                relays[h].start()

    for g in range(chunks):
        y_all[g * chunk : (g + 1) * chunk, :] = within(g, skips)

    gain_a = gain_a_ref[...]
    across = [
        [exchange(send1.at[k], recv1.at[k], k * HALVES + h, (h,)) for k in range(STAGES)]
        for h in range(HALVES)
    ]
    for h in range(HALVES):

        @pl.when(my_col > 0)
        def _():
            relays[h].wait_recv()

            @pl.when(my_col < n_cols - 1)
            def _():
                for g in rows_of(h):
                    state_out[g] = (
                        pushed_all[g] + jnp.exp(l_end[g]) * state_in[g].astype(f32)
                    ).astype(bf16)
                relays[h].start()

        parts = []
        for g in rows_of(h):
            rows = slice(g * chunk, (g + 1) * chunk)
            y = y_all[rows, :] + mm(c_all[rows, :], state_in[g]) * jnp.exp(l_exp[rows, :])
            scale = lax.rsqrt(jnp.mean(y * y, axis=-1, keepdims=True) + 1e-5)
            parts.append((y * scale * gain_a).astype(bf16))
        out_order(send1, h, jnp.concatenate(parts, axis=0))
        for k in range(STAGES):
            across[h][k][0]()

    for h in range(HALVES):
        out_order(ordered, h, masked[half(h), :])
    loads["w_gate"].wait()
    for k in range(STAGES):
        gate = mm(flat(ordered[k]), w_gate_ref[...])
        gated[k * stage_tokens : (k + 1) * stage_tokens, :] = (
            gate / (1.0 + jnp.exp(-gate)) * gain_f_ref[...]
        )
    skips_d = wide(skip_d_ref)
    bias_d, neg_rates_d = tall(bias_d_ref), -tall(rates_d_ref)
    loads["w_down"].wait()
    loads["w_out"].wait()

    @pl.when(my_col < n_cols - 1)
    def _():
        for copy in relays:
            copy.wait_send()

    hand_down = [
        pltpu.make_async_remote_copy(
            src_ref=down_out.at[k],
            dst_ref=down_in.at[k],
            send_sem=down_sems.at[0, k],
            recv_sem=down_sems.at[1, k],
            device_id=(lax.rem(my_row + members, n_rows), my_col),
            device_id_type=MESH,
        )
        for k in range(STAGES)
    ]

    @pl.when(group_of == 0)
    def _():
        down_in[...] = jnp.zeros_like(down_in)

    def ends(k):
        for c in range(stage_lines):
            entered = None
            for i in range(per_line):
                g = k * stage_chunks + c * per_line + i
                end, pushed = push(g)
                if per_line > 1:
                    l_end[g], pushed_all[g] = end, pushed
                entered = pushed if entered is None else jnp.exp(end) * entered + pushed
            down_out[k, c] = entered.astype(bf16)

    for k in range(STAGES):
        for h in range(HALVES):
            across[h][k][1]()
        first_token = k * stage_tokens
        cols = mm(to_columns, flat(recv1[k])).astype(bf16)
        vals[first_token : first_token + stage_tokens, :] = cols
        project(cols, w_down_ref, bias_d, neg_rates_d, first_token)
        if per_line > 1:
            ends(k)

        @pl.when(group_of < GROUPS - 1)
        def _():
            if per_line == 1:
                ends(k)
            hand_down[k].start()

        for g in range(k * stage_chunks, (k + 1) * stage_chunks):
            y_all[g * chunk : (g + 1) * chunk, :] = within(g, skips_d)

    back = [exchange(send2.at[k], recv2.at[k], STAGES * HALVES + k, ()) for k in range(STAGES)]
    for k in range(STAGES):

        @pl.when(group_of > 0)
        def _():
            hand_down[k].wait_recv()

        parts = []
        for c in range(stage_lines):
            entered = down_in[k, c].astype(f32)
            for i in range(per_line):
                g = k * stage_chunks + c * per_line + i
                rows = slice(g * chunk, (g + 1) * chunk)
                extra = mm(c_all[rows, :], entered.astype(bf16)) * jnp.exp(l_exp[rows, :])
                parts.append((y_all[rows, :] + extra).astype(bf16))
                if i < per_line - 1:
                    entered = jnp.exp(l_end[g]) * entered + pushed_all[g]
        send2[k] = shaped(mm_tn(to_columns, jnp.concatenate(parts, axis=0)), send2.shape[1:])
        back[k][0]()

    for k in range(STAGES):
        back[k][1]()
        z = flat(recv2[k]).astype(f32)
        scale = lax.rsqrt(jnp.mean(z * z, axis=-1, keepdims=True) + 1e-5)
        act = z * scale * gated[k * stage_tokens : (k + 1) * stage_tokens, :]
        mixed = flat(ordered[k]).astype(f32) + mm(act.astype(bf16), w_out_ref[...])
        mixed_all[k] = shaped(mixed, mixed_all.shape[1:])
    for h in range(HALVES):
        mixed = mm_tn(by_col, flat(mixed_all[:, :, h])).astype(bf16)
        out_ref[h * half_rows : (h + 1) * half_rows] = mixed.reshape(half_rows, width, feats)

    for h in range(HALVES):
        for k in range(STAGES):
            across[h][k][2]()

    @pl.when(group_of < GROUPS - 1)
    def _():
        for copy in hand_down:
            copy.wait_send()

    for _, _, drain in back:
        drain()


def on_device(n_rows, n_cols, *args):
    args = [a.reshape(1, -1) if a.ndim == 1 else a for a in args]
    args[3], args[4] = args[3].T, args[4].T
    patches = args[0]
    local_rows, width, feats = patches.shape
    tokens = local_rows * width
    heads = args[9].shape[1]
    states = (args[3].shape[0] - heads) // 2
    chunks = local_rows
    members = n_rows // GROUPS
    stage_lines = width // members // STAGES
    piece = (STAGES, members, HALVES, local_rows // HALVES * stage_lines, feats)
    down = (STAGES, stage_lines, states, feats)
    big = (tokens, feats)
    vmem = pl.BlockSpec(memory_space=pltpu.VMEM)
    return pl.pallas_call(
        functools.partial(block_kernel, n_rows, n_cols),
        out_shape=jax.ShapeDtypeStruct(patches.shape, bf16),
        in_specs=[pl.BlockSpec(memory_space=pltpu.HBM)] * len(args),
        out_specs=vmem,
        scratch_shapes=[pltpu.VMEM(a.shape, a.dtype) for a in args]
        + [
            pltpu.VMEM(big, bf16),
            pltpu.VMEM(big, bf16),
            pltpu.VMEM((tokens, states), bf16),
            pltpu.VMEM((tokens, states), bf16),
            pltpu.VMEM((states, tokens), bf16),
            pltpu.VMEM(big, bf16),
            pltpu.VMEM(big, f32),
            pltpu.VMEM(big, f32),
            pltpu.VMEM(big, f32),
            pltpu.VMEM(piece, bf16),
            pltpu.VMEM(piece, bf16),
            pltpu.VMEM((chunks, states, feats), f32),
            pltpu.VMEM((chunks, 1, feats), f32),
            pltpu.VMEM((chunks, states, feats), bf16),
            pltpu.VMEM((chunks, states, feats), bf16),
            pltpu.VMEM(piece, bf16),
            pltpu.VMEM(piece, bf16),
            pltpu.VMEM(piece, bf16),
            pltpu.VMEM(piece, bf16),
            pltpu.SemaphoreType.DMA((STAGES * (HALVES + 1), members)),
            pltpu.SemaphoreType.DMA((STAGES * (HALVES + 1), members)),
            pltpu.SemaphoreType.DMA((2, HALVES)),
            pltpu.VMEM(down, bf16),
            pltpu.VMEM(down, bf16),
            pltpu.SemaphoreType.DMA((2, STAGES)),
            pltpu.SemaphoreType.DMA((len(args),)),
        ],
        compiler_params=pltpu.CompilerParams(
            collective_id=0, has_side_effects=True, vmem_limit_bytes=32 * 1024 * 1024
        ),
    )(*args)


def solution(mesh):
    rep = P()
    return jax.shard_map(
        functools.partial(on_device, mesh.shape["rows"], mesh.shape["cols"]),
        mesh=mesh,
        in_specs=(P("rows", "cols", None), P("rows", "cols")) + (rep,) * 13,
        out_specs=P("rows", "cols", None),
        check_vma=False,
    )
```

```python
import functools

import jax
import jax.numpy as jnp
from jax import lax
from jax.experimental import pallas as pl
from jax.experimental.pallas import tpu as pltpu
from jax.sharding import PartitionSpec as P

MESH = pl.DeviceIdType.MESH
GROUPS = 2
MOST_STAGES = 2
HALVES = 2
f32 = jnp.float32
bf16 = jnp.bfloat16


def mm(a, b):
    return jnp.dot(a, b, preferred_element_type=f32)


def mm_nt(a, b):
    return lax.dot_general(a, b, (((1,), (1,)), ((), ())), preferred_element_type=f32)


def mm_tn(a, b):
    return lax.dot_general(a, b, (((0,), (0,)), ((), ())), preferred_element_type=f32)


def parts_of(x):
    high = x.astype(bf16)
    return high, (x - high.astype(f32)).astype(bf16)


def mm_split_right(a, x):
    high, low = parts_of(x)
    return mm(a, high) + mm(a, low)


def mm_split_left(x, b):
    high, low = parts_of(x)
    return mm(high, b) + mm(low, b)


def iota(shape, dim):
    return lax.broadcasted_iota(jnp.int32, shape, dim)


def log2_of(size):
    assert size & (size - 1) == 0
    return size.bit_length() - 1


def one_hot(index):
    count, lanes = index.shape
    lane = iota(index.shape, 1)
    tiles = [
        jnp.where(index - start == lane, 1.0, 0.0).astype(bf16)
        for start in range(0, count, lanes)
    ]
    return jnp.concatenate(tiles, axis=1)


ARGS = (
    "patches",
    "tissue",
    "w_value",
    "w_across",
    "w_down",
    "w_gate",
    "w_out",
    "bias_a",
    "bias_d",
    "rates_a",
    "rates_d",
    "skip_a",
    "skip_d",
    "gain_a",
    "gain_f",
)
SMALL = ARGS[7:]
LOAD_ORDER = ("tissue", "patches", "w_value", "w_across") + SMALL + ("w_gate", "w_down", "w_out")


def block_kernel(
    n_rows,
    n_cols,
    *refs,
):
    count = len(ARGS)
    sources, out_ref, held = refs[:count], refs[count], refs[count + 1 : 2 * count + 1]
    (
        masked,
        vals,
        b_all,
        c_all,
        bt_all,
        v_all,
        l_exp,
        y_all,
        gated,
        ordered,
        mixed_all,
        pushed_all,
        l_end,
        state_out,
        state_in,
        send1,
        recv1,
        send2,
        recv2,
        send_sems,
        recv_sems,
        relay_sems,
        down_out,
        down_in,
        down_sems,
        load_sems,
    ) = refs[2 * count + 1 :]
    loads = {
        name: pltpu.make_async_copy(sources[k], held[k], load_sems.at[k])
        for k, name in enumerate(ARGS)
        if name != "patches"
    }
    half_rows = sources[0].shape[0] // HALVES
    patch_loads = [
        pltpu.make_async_copy(
            sources[0].at[pl.ds(h * half_rows, half_rows)],
            held[0].at[pl.ds(h * half_rows, half_rows)],
            load_sems.at[count + h],
        )
        for h in range(HALVES)
    ]
    for name in LOAD_ORDER:
        if name == "patches":
            for load in patch_loads:
                load.start()
        else:
            loads[name].start()
    (
        patches_ref,
        tissue_ref,
        w_value_ref,
        w_across_ref,
        w_down_ref,
        w_gate_ref,
        w_out_ref,
        bias_a_ref,
        bias_d_ref,
        rates_a_ref,
        rates_d_ref,
        skip_a_ref,
        skip_d_ref,
        gain_a_ref,
        gain_f_ref,
    ) = held
    local_rows, width, feats = patches_ref.shape
    heads = rates_a_ref.shape[1]
    head_width = feats // heads
    states = (w_across_ref.shape[0] - heads) // 2
    tokens = local_rows * width
    chunk = width
    chunks = tokens // chunk
    members = n_rows // GROUPS
    per_peer = width // members
    height = members * local_rows
    stages = min(MOST_STAGES, per_peer)
    stage_tokens = tokens // stages
    stage_chunks = chunks // stages
    half_tokens = tokens // HALVES
    stage_lines = per_peer // stages
    per_line = height // chunk
    assert head_width == chunk and height % chunk == 0

    my_row = lax.axis_index("rows")
    my_col = lax.axis_index("cols")

    barrier = pltpu.get_barrier_semaphore()

    group_of = my_row // members
    member = lax.rem(my_row, members)
    base = group_of * members

    def fellow(off):
        return lax.rem(member + off, members)

    def each_fellow(body):
        if members <= 8:
            for off in range(1, members):
                body(off)
        else:
            pl.loop(1, members)(body)

    @each_fellow
    def _(off):
        pl.semaphore_signal(
            barrier, inc=1, device_id=(base + fellow(off), my_col), device_id_type=MESH
        )

    @pl.when(group_of > 0)
    def _():
        pl.semaphore_signal(
            barrier, inc=1, device_id=(my_row - members, my_col), device_id_type=MESH
        )

    @pl.when(my_col > 0)
    def _():
        pl.semaphore_signal(
            barrier, inc=1, device_id=(my_row, my_col - 1), device_id_type=MESH
        )

    lane = iota((heads, feats), 1)
    first = iota((heads, feats), 0) * head_width
    expand = jnp.where((lane >= first) & (lane < first + head_width), 1.0, 0.0).astype(bf16)
    place_t = iota((chunk, feats), 0)
    place_u = iota((chunk, feats), 1) & (head_width - 1)
    causal = place_t >= place_u
    diagonal = place_t == place_u
    pair = 2 if stage_chunks % 2 == 0 else 1
    span = pair * chunk
    tri_t, tri_u = iota((span, span), 0), iota((span, span), 1)
    csh = log2_of(chunk)
    tri = jnp.where(
        (tri_t >= tri_u)
        & (lax.shift_right_logical(tri_t, csh) == lax.shift_right_logical(tri_u, csh)),
        1.0,
        0.0,
    ).astype(bf16)
    tri = jnp.concatenate([tri, tri], axis=1)
    group = min(heads, 4)
    gw = group * head_width
    sh = log2_of(head_width)
    same_head = jnp.where(
        lax.shift_right_logical(iota((gw, gw), 0), sh)
        == lax.shift_right_logical(iota((gw, gw), 1), sh),
        1.0,
        0.0,
    ).astype(bf16)

    def wide(ref):
        return mm_split_left(jnp.broadcast_to(ref[...], (8, heads)), expand)[0:1]

    def tall(ref):
        square = jnp.broadcast_to(ref[...], (heads, heads))
        eye = iota((heads, heads), 0) == iota((heads, heads), 1)
        return jnp.sum(jnp.where(eye, square, 0.0), axis=1, keepdims=True)

    def spread(x):
        high, low = parts_of(x)
        return mm_tn(
            jnp.concatenate([high, low], axis=0), jnp.concatenate([expand, expand], axis=0)
        )

    def project(x, w_ref, bias, neg_rates, start=0):
        here = slice(start, start + x.shape[0])
        weights = w_ref[...]
        proj = mm_nt(x, weights[: 2 * states])
        b_all[here, :] = proj[:, :states].astype(bf16)
        c_all[here, :] = proj[:, states:].astype(bf16)
        turned = mm_nt(weights, x)
        bt_all[:, here] = turned[:states].astype(bf16)
        v = turned[2 * states :] + bias
        steps = jnp.maximum(v, 0.0) + jnp.log1p(jnp.exp(-jnp.abs(v)))
        v_all[here, :] = (spread(steps) * vals[here, :].astype(f32)).astype(bf16)
        high, low = parts_of(spread(steps * neg_rates))
        for g in range(0, x.shape[0], span):
            rows = slice(g, g + span)
            l_exp[start + g : start + g + span, :] = mm(tri, jnp.concatenate([high[rows], low[rows]], axis=0))

    def push(g):
        rows = slice(g * chunk, (g + 1) * chunk)
        run = l_exp[rows, :]
        end = run[chunk - 1 : chunk, :]
        scaled = v_all[rows, :].astype(f32) * jnp.exp(end - run)
        return end, mm(bt_all[:, rows], scaled.astype(bf16))

    def within(g, skips):
        rows = slice(g * chunk, (g + 1) * chunk)
        run = l_exp[rows, :]
        run_u = jnp.sum(jnp.where(diagonal, run, 0.0), axis=0, keepdims=True)
        b = b_all[rows, :]
        cb = mm_nt(c_all[rows, :], jnp.concatenate([b] * heads, axis=0))
        decay = jnp.exp(jnp.where(causal, run - run_u, -1e30))
        weights = (decay * cb).astype(bf16)
        vb = v_all[rows, :]
        outs = []
        for q in range(heads // group):
            lanes = slice(q * gw, (q + 1) * gw)
            stacked = jnp.concatenate([vb[:, lanes]] * group, axis=0) * same_head
            outs.append(mm(weights[:, lanes], stacked))
        return jnp.concatenate(outs, axis=1) + skips * vals[rows, :].astype(f32)

    def exchange(source, target, sems, part):
        def copy_of(off, to, place):
            return pltpu.make_async_remote_copy(
                src_ref=source.at[(to,) + part],
                dst_ref=target.at[(place,) + part],
                send_sem=send_sems.at[sems, off],
                recv_sem=recv_sems.at[sems, off],
                device_id=(base + to, my_col),
                device_id_type=MESH,
            )

        def start():
            @each_fellow
            def _(off):
                copy_of(off, fellow(off), member).start()

            target[(member,) + part] = source[(member,) + part]

        def finish():
            @each_fellow
            def _(off):
                came = fellow(members - off)
                copy_of(off, came, came).wait_recv()

        def drain():
            @each_fellow
            def _(off):
                copy_of(off, fellow(off), member).wait_send()

        return start, finish, drain

    def shaped(x, shape):
        if shape[-2] % 16:
            return x.astype(f32).reshape(shape).astype(bf16)
        return x.astype(bf16).reshape(shape)

    def flat(x):
        if x.shape[-2] % 16:
            return x.astype(f32).reshape(-1, feats).astype(bf16)
        return x.reshape(-1, feats)

    rsh = log2_of(half_rows)
    hsh = log2_of(height)
    lsh = log2_of(stage_lines)
    msh = log2_of(members)
    shr = lax.shift_right_logical
    m = iota((half_tokens, 128), 0)
    by_col = one_hot(
        ((m & (half_rows - 1)) << csh)
        + ((shr(m, rsh + lsh) & (members - 1)) << log2_of(per_peer))
        + (shr(m, rsh + lsh + msh) << lsh)
        + (shr(m, rsh) & (stage_lines - 1))
    )
    m = iota((stage_tokens, 128), 0)
    i_of = m & (height - 1)
    to_columns = one_hot(
        (shr(i_of, rsh) << (rsh + lsh)) + (shr(m, hsh) << rsh) + (i_of & (half_rows - 1))
    )

    def half(h):
        return slice(h * half_tokens, (h + 1) * half_tokens)

    def out_order(ref, h, x):
        x = mm(by_col, x)
        ref[:, :, h] = shaped(x, (stages, members) + ref.shape[3:])

    loads["tissue"].wait()
    flags = tissue_ref[...].astype(f32).T
    for name in ("w_value", "w_across") + SMALL:
        loads[name].wait()
    bias_a, neg_rates_a = tall(bias_a_ref), -tall(rates_a_ref)
    relays = [
        pltpu.make_async_remote_copy(
            src_ref=state_out.at[pl.ds(h * half_rows, half_rows)],
            dst_ref=state_in.at[pl.ds(h * half_rows, half_rows)],
            send_sem=relay_sems.at[0, h],
            recv_sem=relay_sems.at[1, h],
            device_id=(my_row, lax.rem(my_col + 1, n_cols)),
            device_id_type=MESH,
        )
        for h in range(HALVES)
    ]

    def rows_of(h):
        return range(h * half_rows, (h + 1) * half_rows)

    greeted = (
        members
        - 1
        + jnp.where(my_col < n_cols - 1, 1, 0)
        + jnp.where(group_of < GROUPS - 1, 1, 0)
    )

    @pl.when(my_col == 0)
    def _():
        state_in[...] = jnp.zeros_like(state_in)

    for h in range(HALVES):
        patch_loads[h].wait()
        for r in rows_of(h):
            flag = jnp.broadcast_to(flags[:, r : r + 1], (width, feats)) > 0.5
            masked[r * width : (r + 1) * width, :] = jnp.where(
                flag, patches_ref[r].astype(f32), 0.0
            ).astype(bf16)
        x = masked[half(h), :]
        vals[half(h), :] = mm(x, w_value_ref[...]).astype(bf16)
        project(x, w_across_ref, bias_a, neg_rates_a, h * half_tokens)

        @pl.when(my_col < n_cols - 1)
        def _():
            for g in rows_of(h):
                end, pushed = push(g)
                state_out[g] = pushed.astype(bf16)
                if n_cols > 2:
                    l_end[g], pushed_all[g] = end, pushed

        if h == 0:
            pl.semaphore_wait(barrier, greeted)

        if n_cols > 1:

            @pl.when(my_col == 0)
            def _():
                relays[h].start()

    skips = wide(skip_a_ref)

    for g in range(chunks):
        y_all[g * chunk : (g + 1) * chunk, :] = within(g, skips)

    def pass_on(h):
        @pl.when(my_col < n_cols - 1)
        def _():
            for g in rows_of(h):
                state_out[g] = (
                    pushed_all[g] + jnp.exp(l_end[g]) * state_in[g].astype(f32)
                ).astype(bf16)
            relays[h].start()

    gain_a = gain_a_ref[...]
    across = [
        [exchange(send1.at[k], recv1.at[k], k * HALVES + h, (h,)) for k in range(stages)]
        for h in range(HALVES)
    ]
    for h in range(HALVES):

        @pl.when(my_col > 0)
        def _():
            relays[h].wait_recv()

            if n_cols > 2:
                pass_on(h)

        parts = []
        for g in rows_of(h):
            rows = slice(g * chunk, (g + 1) * chunk)
            y = y_all[rows, :] + mm(c_all[rows, :], state_in[g]) * jnp.exp(l_exp[rows, :])
            scale = lax.rsqrt(jnp.mean(y * y, axis=-1, keepdims=True) + 1e-5)
            parts.append((y * scale * gain_a).astype(bf16))
        out_order(send1, h, jnp.concatenate(parts, axis=0))
        for k in range(stages):
            across[h][k][0]()

    for h in range(HALVES):
        out_order(ordered, h, masked[half(h), :])
    loads["w_gate"].wait()
    for k in range(stages):
        gate = mm(flat(ordered[k]), w_gate_ref[...])
        gated[k * stage_tokens : (k + 1) * stage_tokens, :] = (
            gate / (1.0 + jnp.exp(-gate)) * gain_f_ref[...]
        )
    skips_d = wide(skip_d_ref)
    bias_d, neg_rates_d = tall(bias_d_ref), -tall(rates_d_ref)
    loads["w_down"].wait()
    loads["w_out"].wait()

    @pl.when(my_col < n_cols - 1)
    def _():
        for copy in relays:
            copy.wait_send()

    hand_down = [
        pltpu.make_async_remote_copy(
            src_ref=down_out.at[k],
            dst_ref=down_in.at[k],
            send_sem=down_sems.at[0, k],
            recv_sem=down_sems.at[1, k],
            device_id=(lax.rem(my_row + members, n_rows), my_col),
            device_id_type=MESH,
        )
        for k in range(stages)
    ]

    @pl.when(group_of == 0)
    def _():
        down_in[...] = jnp.zeros_like(down_in)

    def ends(k):
        for c in range(stage_lines):
            entered = None
            for i in range(per_line):
                g = k * stage_chunks + c * per_line + i
                end, pushed = push(g)
                if per_line > 1:
                    l_end[g], pushed_all[g] = end, pushed
                entered = pushed if entered is None else jnp.exp(end) * entered + pushed
            down_out[k, c] = entered.astype(bf16)

    for k in range(stages):
        for h in range(HALVES):
            across[h][k][1]()
        first_token = k * stage_tokens
        cols = mm(to_columns, flat(recv1[k])).astype(bf16)
        vals[first_token : first_token + stage_tokens, :] = cols
        project(cols, w_down_ref, bias_d, neg_rates_d, first_token)
        if per_line > 1:
            ends(k)

        @pl.when(group_of < GROUPS - 1)
        def _():
            if per_line == 1:
                ends(k)
            hand_down[k].start()

        for g in range(k * stage_chunks, (k + 1) * stage_chunks):
            y_all[g * chunk : (g + 1) * chunk, :] = within(g, skips_d)

    back = [exchange(send2.at[k], recv2.at[k], stages * HALVES + k, ()) for k in range(stages)]
    for k in range(stages):

        @pl.when(group_of > 0)
        def _():
            hand_down[k].wait_recv()

        parts = []
        for c in range(stage_lines):
            entered = down_in[k, c].astype(f32)
            for i in range(per_line):
                g = k * stage_chunks + c * per_line + i
                rows = slice(g * chunk, (g + 1) * chunk)
                extra = mm(c_all[rows, :], entered.astype(bf16)) * jnp.exp(l_exp[rows, :])
                parts.append((y_all[rows, :] + extra).astype(bf16))
                if i < per_line - 1:
                    entered = jnp.exp(l_end[g]) * entered + pushed_all[g]
        send2[k] = shaped(mm_tn(to_columns, jnp.concatenate(parts, axis=0)), send2.shape[1:])
        back[k][0]()

    for k in range(stages):
        back[k][1]()
        z = flat(recv2[k]).astype(f32)
        scale = lax.rsqrt(jnp.mean(z * z, axis=-1, keepdims=True) + 1e-5)
        act = z * scale * gated[k * stage_tokens : (k + 1) * stage_tokens, :]
        mixed = flat(ordered[k]).astype(f32) + mm(act.astype(bf16), w_out_ref[...])
        mixed_all[k] = shaped(mixed, mixed_all.shape[1:])
    for h in range(HALVES):
        mixed = mm_tn(by_col, flat(mixed_all[:, :, h])).astype(bf16)
        out_ref[h * half_rows : (h + 1) * half_rows] = mixed.reshape(half_rows, width, feats)

    for h in range(HALVES):
        for k in range(stages):
            across[h][k][2]()

    @pl.when(group_of < GROUPS - 1)
    def _():
        for copy in hand_down:
            copy.wait_send()

    for _, _, drain in back:
        drain()


def on_device(n_rows, n_cols, *args):
    args = [a.reshape(1, -1) if a.ndim == 1 else a for a in args]
    args[3], args[4] = args[3].T, args[4].T
    patches = args[0]
    local_rows, width, feats = patches.shape
    tokens = local_rows * width
    heads = args[9].shape[1]
    states = (args[3].shape[0] - heads) // 2
    chunks = local_rows
    members = n_rows // GROUPS
    stages = min(MOST_STAGES, width // members)
    stage_lines = width // members // stages
    piece = (stages, members, HALVES, local_rows // HALVES * stage_lines, feats)
    down = (stages, stage_lines, states, feats)
    big = (tokens, feats)
    vmem = pl.BlockSpec(memory_space=pltpu.VMEM)
    return pl.pallas_call(
        functools.partial(block_kernel, n_rows, n_cols),
        out_shape=jax.ShapeDtypeStruct(patches.shape, bf16),
        in_specs=[pl.BlockSpec(memory_space=pltpu.HBM)] * len(args),
        out_specs=vmem,
        scratch_shapes=[pltpu.VMEM(a.shape, a.dtype) for a in args]
        + [
            pltpu.VMEM(big, bf16),
            pltpu.VMEM(big, bf16),
            pltpu.VMEM((tokens, states), bf16),
            pltpu.VMEM((tokens, states), bf16),
            pltpu.VMEM((states, tokens), bf16),
            pltpu.VMEM(big, bf16),
            pltpu.VMEM(big, f32),
            pltpu.VMEM(big, f32),
            pltpu.VMEM(big, f32),
            pltpu.VMEM(piece, bf16),
            pltpu.VMEM(piece, bf16),
            pltpu.VMEM((chunks, states, feats), f32),
            pltpu.VMEM((chunks, 1, feats), f32),
            pltpu.VMEM((chunks, states, feats), bf16),
            pltpu.VMEM((chunks, states, feats), bf16),
            pltpu.VMEM(piece, bf16),
            pltpu.VMEM(piece, bf16),
            pltpu.VMEM(piece, bf16),
            pltpu.VMEM(piece, bf16),
            pltpu.SemaphoreType.DMA((stages * (HALVES + 1), members)),
            pltpu.SemaphoreType.DMA((stages * (HALVES + 1), members)),
            pltpu.SemaphoreType.DMA((2, HALVES)),
            pltpu.VMEM(down, bf16),
            pltpu.VMEM(down, bf16),
            pltpu.SemaphoreType.DMA((2, stages)),
            pltpu.SemaphoreType.DMA((len(args) + HALVES,)),
        ],
        compiler_params=pltpu.CompilerParams(
            collective_id=0, has_side_effects=True, vmem_limit_bytes=425 * 128 * 1024
        ),
    )(*args)


def solution(mesh):
    rep = P()
    return jax.shard_map(
        functools.partial(on_device, mesh.shape["rows"], mesh.shape["cols"]),
        mesh=mesh,
        in_specs=(P("rows", "cols", None), P("rows", "cols")) + (rep,) * 13,
        out_specs=P("rows", "cols", None),
        check_vma=False,
    )
```

```python
import functools

import jax
import jax.numpy as jnp
from jax import lax
from jax.experimental import pallas as pl
from jax.experimental.pallas import tpu as pltpu
from jax.sharding import PartitionSpec as P

MESH = pl.DeviceIdType.MESH
GROUPS = 2
MOST_STAGES = 2
HALVES = 2
f32 = jnp.float32
bf16 = jnp.bfloat16


def mm(a, b):
    return jnp.dot(a, b, preferred_element_type=f32)


def mm_nt(a, b):
    return lax.dot_general(a, b, (((1,), (1,)), ((), ())), preferred_element_type=f32)


def mm_tn(a, b):
    return lax.dot_general(a, b, (((0,), (0,)), ((), ())), preferred_element_type=f32)


def parts_of(x):
    high = x.astype(bf16)
    return high, (x - high.astype(f32)).astype(bf16)


def mm_split_right(a, x):
    high, low = parts_of(x)
    return mm(a, high) + mm(a, low)


def mm_split_left(x, b):
    high, low = parts_of(x)
    return mm(high, b) + mm(low, b)


def iota(shape, dim):
    return lax.broadcasted_iota(jnp.int32, shape, dim)


def log2_of(size):
    assert size & (size - 1) == 0
    return size.bit_length() - 1


def one_hot(index):
    count, lanes = index.shape
    lane = iota(index.shape, 1)
    tiles = [
        jnp.where(index - start == lane, 1.0, 0.0).astype(bf16)
        for start in range(0, count, lanes)
    ]
    return jnp.concatenate(tiles, axis=1)


ARGS = (
    "patches",
    "tissue",
    "w_value",
    "w_across",
    "w_down",
    "w_gate",
    "w_out",
    "bias_a",
    "bias_d",
    "rates_a",
    "rates_d",
    "skip_a",
    "skip_d",
    "gain_a",
    "gain_f",
)
SMALL = ARGS[7:]
LOAD_ORDER = ("tissue", "patches", "w_value", "w_across") + SMALL + ("w_gate", "w_down", "w_out")


def block_kernel(
    n_rows,
    n_cols,
    *refs,
):
    count = len(ARGS)
    sources, out_ref, held = refs[:count], refs[count], refs[count + 1 : 2 * count + 1]
    (
        masked,
        vals,
        b_all,
        c_all,
        bt_all,
        v_all,
        l_exp,
        y_all,
        gated,
        ordered,
        mixed_all,
        pushed_all,
        l_end,
        state_out,
        state_in,
        send1,
        recv1,
        send2,
        recv2,
        send_sems,
        recv_sems,
        relay_sems,
        down_out,
        down_in,
        down_sems,
        load_sems,
    ) = refs[2 * count + 1 :]
    loads = {
        name: pltpu.make_async_copy(sources[k], held[k], load_sems.at[k])
        for k, name in enumerate(ARGS)
        if name != "patches"
    }
    half_rows = sources[0].shape[0] // HALVES
    patch_loads = [
        pltpu.make_async_copy(
            sources[0].at[pl.ds(h * half_rows, half_rows)],
            held[0].at[pl.ds(h * half_rows, half_rows)],
            load_sems.at[count + h],
        )
        for h in range(HALVES)
    ]
    for name in LOAD_ORDER:
        if name == "patches":
            for load in patch_loads:
                load.start()
        else:
            loads[name].start()
    (
        patches_ref,
        tissue_ref,
        w_value_ref,
        w_across_ref,
        w_down_ref,
        w_gate_ref,
        w_out_ref,
        bias_a_ref,
        bias_d_ref,
        rates_a_ref,
        rates_d_ref,
        skip_a_ref,
        skip_d_ref,
        gain_a_ref,
        gain_f_ref,
    ) = held
    local_rows, width, feats = patches_ref.shape
    heads = rates_a_ref.shape[1]
    head_width = feats // heads
    states = (w_across_ref.shape[0] - heads) // 2
    tokens = local_rows * width
    chunk = width
    chunks = tokens // chunk
    members = n_rows // GROUPS
    per_peer = width // members
    height = members * local_rows
    stages = min(MOST_STAGES, per_peer)
    stage_tokens = tokens // stages
    stage_chunks = chunks // stages
    half_tokens = tokens // HALVES
    stage_lines = per_peer // stages
    per_line = height // chunk
    assert head_width == chunk and height % chunk == 0

    my_row = lax.axis_index("rows")
    my_col = lax.axis_index("cols")

    barrier = pltpu.get_barrier_semaphore()

    group_of = my_row // members
    member = lax.rem(my_row, members)
    base = group_of * members

    def fellow(off):
        return lax.rem(member + off, members)

    def each_fellow(body):
        if members <= 8:
            for off in range(1, members):
                body(off)
        else:
            pl.loop(1, members)(body)

    @each_fellow
    def _(off):
        pl.semaphore_signal(
            barrier, inc=1, device_id=(base + fellow(off), my_col), device_id_type=MESH
        )

    @pl.when(group_of > 0)
    def _():
        pl.semaphore_signal(
            barrier, inc=1, device_id=(my_row - members, my_col), device_id_type=MESH
        )

    @pl.when(my_col > 0)
    def _():
        pl.semaphore_signal(
            barrier, inc=1, device_id=(my_row, my_col - 1), device_id_type=MESH
        )

    lane = iota((heads, feats), 1)
    first = iota((heads, feats), 0) * head_width
    expand = jnp.where((lane >= first) & (lane < first + head_width), 1.0, 0.0).astype(bf16)
    place_t = iota((chunk, feats), 0)
    place_u = iota((chunk, feats), 1) & (head_width - 1)
    causal = place_t >= place_u
    diagonal = place_t == place_u
    pair = 2 if stage_chunks % 2 == 0 else 1
    span = pair * chunk
    tri_t, tri_u = iota((span, span), 0), iota((span, span), 1)
    csh = log2_of(chunk)
    tri = jnp.where(
        (tri_t >= tri_u)
        & (lax.shift_right_logical(tri_t, csh) == lax.shift_right_logical(tri_u, csh)),
        1.0,
        0.0,
    ).astype(bf16)
    tri = jnp.concatenate([tri, tri], axis=1)
    group = min(heads, 4)
    gw = group * head_width
    sh = log2_of(head_width)
    same_head = jnp.where(
        lax.shift_right_logical(iota((gw, gw), 0), sh)
        == lax.shift_right_logical(iota((gw, gw), 1), sh),
        1.0,
        0.0,
    ).astype(bf16)

    def wide(ref):
        return mm_split_left(jnp.broadcast_to(ref[...], (8, heads)), expand)[0:1]

    def tall(ref):
        square = jnp.broadcast_to(ref[...], (heads, heads))
        eye = iota((heads, heads), 0) == iota((heads, heads), 1)
        return jnp.sum(jnp.where(eye, square, 0.0), axis=1, keepdims=True)

    def spread(x):
        high, low = parts_of(x)
        return mm_tn(
            jnp.concatenate([high, low], axis=0), jnp.concatenate([expand, expand], axis=0)
        )

    def project(x, w_ref, bias, neg_rates, start=0):
        here = slice(start, start + x.shape[0])
        weights = w_ref[...]
        proj = mm_nt(x, weights[: 2 * states])
        b_all[here, :] = proj[:, :states].astype(bf16)
        c_all[here, :] = proj[:, states:].astype(bf16)
        turned = mm_nt(weights, x)
        bt_all[:, here] = turned[:states].astype(bf16)
        v = turned[2 * states :] + bias
        steps = jnp.maximum(v, 0.0) + jnp.log1p(jnp.exp(-jnp.abs(v)))
        v_all[here, :] = (spread(steps) * vals[here, :].astype(f32)).astype(bf16)
        high, low = parts_of(spread(steps * neg_rates))
        for g in range(0, x.shape[0], span):
            rows = slice(g, g + span)
            l_exp[start + g : start + g + span, :] = mm(tri, jnp.concatenate([high[rows], low[rows]], axis=0))

    def push(g):
        rows = slice(g * chunk, (g + 1) * chunk)
        run = l_exp[rows, :]
        end = run[chunk - 1 : chunk, :]
        scaled = v_all[rows, :].astype(f32) * jnp.exp(end - run)
        return end, mm(bt_all[:, rows], scaled.astype(bf16))

    def within(g, skips):
        rows = slice(g * chunk, (g + 1) * chunk)
        run = l_exp[rows, :]
        run_u = jnp.sum(jnp.where(diagonal, run, 0.0), axis=0, keepdims=True)
        b = b_all[rows, :]
        cb = mm_nt(c_all[rows, :], jnp.concatenate([b, b], axis=0))
        cb = jnp.concatenate([cb] * (heads // 2), axis=1)
        decay = jnp.exp(jnp.where(causal, run - run_u, -1e30))
        weights = (decay * cb).astype(bf16)
        vb = v_all[rows, :]
        outs = []
        for q in range(heads // group):
            lanes = slice(q * gw, (q + 1) * gw)
            stacked = jnp.concatenate([vb[:, lanes]] * group, axis=0) * same_head
            outs.append(mm(weights[:, lanes], stacked))
        return jnp.concatenate(outs, axis=1) + skips * vals[rows, :].astype(f32)

    def exchange(source, target, sems, part):
        def copy_of(off, to, place):
            return pltpu.make_async_remote_copy(
                src_ref=source.at[(to,) + part],
                dst_ref=target.at[(place,) + part],
                send_sem=send_sems.at[sems, off],
                recv_sem=recv_sems.at[sems, off],
                device_id=(base + to, my_col),
                device_id_type=MESH,
            )

        def start():
            @each_fellow
            def _(off):
                copy_of(off, fellow(off), member).start()

            target[(member,) + part] = source[(member,) + part]

        def finish():
            @each_fellow
            def _(off):
                came = fellow(members - off)
                copy_of(off, came, came).wait_recv()

        def drain():
            @each_fellow
            def _(off):
                copy_of(off, fellow(off), member).wait_send()

        return start, finish, drain

    def shaped(x, shape):
        if shape[-2] % 16:
            return x.astype(f32).reshape(shape).astype(bf16)
        return x.astype(bf16).reshape(shape)

    def flat(x):
        if x.shape[-2] % 16:
            return x.astype(f32).reshape(-1, feats).astype(bf16)
        return x.reshape(-1, feats)

    rsh = log2_of(half_rows)
    hsh = log2_of(height)
    lsh = log2_of(stage_lines)
    msh = log2_of(members)
    shr = lax.shift_right_logical
    m = iota((half_tokens, 128), 0)
    by_col = one_hot(
        ((m & (half_rows - 1)) << csh)
        + ((shr(m, rsh + lsh) & (members - 1)) << log2_of(per_peer))
        + (shr(m, rsh + lsh + msh) << lsh)
        + (shr(m, rsh) & (stage_lines - 1))
    )
    m = iota((stage_tokens, 128), 0)
    i_of = m & (height - 1)
    to_columns = one_hot(
        (shr(i_of, rsh) << (rsh + lsh)) + (shr(m, hsh) << rsh) + (i_of & (half_rows - 1))
    )

    def half(h):
        return slice(h * half_tokens, (h + 1) * half_tokens)

    def out_order(ref, h, x):
        x = mm(by_col, x)
        ref[:, :, h] = shaped(x, (stages, members) + ref.shape[3:])

    loads["tissue"].wait()
    flags = tissue_ref[...].astype(f32).T
    for name in ("w_value", "w_across") + SMALL:
        loads[name].wait()
    bias_a, neg_rates_a = tall(bias_a_ref), -tall(rates_a_ref)
    relays = [
        pltpu.make_async_remote_copy(
            src_ref=state_out.at[pl.ds(h * half_rows, half_rows)],
            dst_ref=state_in.at[pl.ds(h * half_rows, half_rows)],
            send_sem=relay_sems.at[0, h],
            recv_sem=relay_sems.at[1, h],
            device_id=(my_row, lax.rem(my_col + 1, n_cols)),
            device_id_type=MESH,
        )
        for h in range(HALVES)
    ]

    def rows_of(h):
        return range(h * half_rows, (h + 1) * half_rows)

    greeted = (
        members
        - 1
        + jnp.where(my_col < n_cols - 1, 1, 0)
        + jnp.where(group_of < GROUPS - 1, 1, 0)
    )

    @pl.when(my_col == 0)
    def _():
        state_in[...] = jnp.zeros_like(state_in)

    for h in range(HALVES):
        patch_loads[h].wait()
        for r in rows_of(h):
            flag = jnp.broadcast_to(flags[:, r : r + 1], (width, feats)) > 0.5
            masked[r * width : (r + 1) * width, :] = jnp.where(
                flag, patches_ref[r].astype(f32), 0.0
            ).astype(bf16)
        x = masked[half(h), :]
        vals[half(h), :] = mm(x, w_value_ref[...]).astype(bf16)
        project(x, w_across_ref, bias_a, neg_rates_a, h * half_tokens)

        @pl.when(my_col < n_cols - 1)
        def _():
            for g in rows_of(h):
                end, pushed = push(g)
                state_out[g] = pushed.astype(bf16)
                if n_cols > 2:
                    l_end[g], pushed_all[g] = end, pushed

        if h == 0:
            pl.semaphore_wait(barrier, greeted)

        if n_cols > 1:

            @pl.when(my_col == 0)
            def _():
                relays[h].start()

    skips = wide(skip_a_ref)

    for g in range(chunks):
        y_all[g * chunk : (g + 1) * chunk, :] = within(g, skips)

    def pass_on(h):
        @pl.when(my_col < n_cols - 1)
        def _():
            for g in rows_of(h):
                state_out[g] = (
                    pushed_all[g] + jnp.exp(l_end[g]) * state_in[g].astype(f32)
                ).astype(bf16)
            relays[h].start()

    gain_a = gain_a_ref[...]
    across = [
        [exchange(send1.at[k], recv1.at[k], k * HALVES + h, (h,)) for k in range(stages)]
        for h in range(HALVES)
    ]
    for h in range(HALVES):

        @pl.when(my_col > 0)
        def _():
            relays[h].wait_recv()

            if n_cols > 2:
                pass_on(h)

        parts = []
        for g in rows_of(h):
            rows = slice(g * chunk, (g + 1) * chunk)
            y = y_all[rows, :] + mm(c_all[rows, :], state_in[g]) * jnp.exp(l_exp[rows, :])
            scale = lax.rsqrt(jnp.mean(y * y, axis=-1, keepdims=True) + 1e-5)
            parts.append((y * scale * gain_a).astype(bf16))
        out_order(send1, h, jnp.concatenate(parts, axis=0))
        for k in range(stages):
            across[h][k][0]()

    for h in range(HALVES):
        out_order(ordered, h, masked[half(h), :])
    loads["w_gate"].wait()
    for k in range(stages):
        gate = mm(flat(ordered[k]), w_gate_ref[...])
        gated[k * stage_tokens : (k + 1) * stage_tokens, :] = (
            gate / (1.0 + jnp.exp(-gate)) * gain_f_ref[...]
        )
    skips_d = wide(skip_d_ref)
    bias_d, neg_rates_d = tall(bias_d_ref), -tall(rates_d_ref)
    loads["w_down"].wait()
    loads["w_out"].wait()

    @pl.when(my_col < n_cols - 1)
    def _():
        for copy in relays:
            copy.wait_send()

    hand_down = [
        pltpu.make_async_remote_copy(
            src_ref=down_out.at[k],
            dst_ref=down_in.at[k],
            send_sem=down_sems.at[0, k],
            recv_sem=down_sems.at[1, k],
            device_id=(lax.rem(my_row + members, n_rows), my_col),
            device_id_type=MESH,
        )
        for k in range(stages)
    ]

    @pl.when(group_of == 0)
    def _():
        down_in[...] = jnp.zeros_like(down_in)

    def ends(k):
        for c in range(stage_lines):
            entered = None
            for i in range(per_line):
                g = k * stage_chunks + c * per_line + i
                end, pushed = push(g)
                if per_line > 1:
                    l_end[g], pushed_all[g] = end, pushed
                entered = pushed if entered is None else jnp.exp(end) * entered + pushed
            down_out[k, c] = entered.astype(bf16)

    for k in range(stages):
        for h in range(HALVES):
            across[h][k][1]()
        first_token = k * stage_tokens
        cols = mm(to_columns, flat(recv1[k])).astype(bf16)
        vals[first_token : first_token + stage_tokens, :] = cols
        project(cols, w_down_ref, bias_d, neg_rates_d, first_token)
        if per_line > 1:
            ends(k)

        @pl.when(group_of < GROUPS - 1)
        def _():
            if per_line == 1:
                ends(k)
            hand_down[k].start()

        for g in range(k * stage_chunks, (k + 1) * stage_chunks):
            y_all[g * chunk : (g + 1) * chunk, :] = within(g, skips_d)

    back = [exchange(send2.at[k], recv2.at[k], stages * HALVES + k, ()) for k in range(stages)]
    for k in range(stages):

        @pl.when(group_of > 0)
        def _():
            hand_down[k].wait_recv()

        parts = []
        for c in range(stage_lines):
            entered = down_in[k, c].astype(f32)
            for i in range(per_line):
                g = k * stage_chunks + c * per_line + i
                rows = slice(g * chunk, (g + 1) * chunk)
                extra = mm(c_all[rows, :], entered.astype(bf16)) * jnp.exp(l_exp[rows, :])
                parts.append((y_all[rows, :] + extra).astype(bf16))
                if i < per_line - 1:
                    entered = jnp.exp(l_end[g]) * entered + pushed_all[g]
        send2[k] = shaped(mm_tn(to_columns, jnp.concatenate(parts, axis=0)), send2.shape[1:])
        back[k][0]()

    for k in range(stages):
        back[k][1]()
        z = flat(recv2[k]).astype(f32)
        scale = lax.rsqrt(jnp.mean(z * z, axis=-1, keepdims=True) + 1e-5)
        act = z * scale * gated[k * stage_tokens : (k + 1) * stage_tokens, :]
        mixed = flat(ordered[k]).astype(f32) + mm(act.astype(bf16), w_out_ref[...])
        mixed_all[k] = shaped(mixed, mixed_all.shape[1:])
    for h in range(HALVES):
        mixed = mm_tn(by_col, flat(mixed_all[:, :, h])).astype(bf16)
        out_ref[h * half_rows : (h + 1) * half_rows] = mixed.reshape(half_rows, width, feats)

    for h in range(HALVES):
        for k in range(stages):
            across[h][k][2]()

    @pl.when(group_of < GROUPS - 1)
    def _():
        for copy in hand_down:
            copy.wait_send()

    for _, _, drain in back:
        drain()


def on_device(n_rows, n_cols, *args):
    args = [a.reshape(1, -1) if a.ndim == 1 else a for a in args]
    args[3], args[4] = args[3].T, args[4].T
    patches = args[0]
    local_rows, width, feats = patches.shape
    tokens = local_rows * width
    heads = args[9].shape[1]
    states = (args[3].shape[0] - heads) // 2
    chunks = local_rows
    members = n_rows // GROUPS
    stages = min(MOST_STAGES, width // members)
    stage_lines = width // members // stages
    piece = (stages, members, HALVES, local_rows // HALVES * stage_lines, feats)
    down = (stages, stage_lines, states, feats)
    big = (tokens, feats)
    vmem = pl.BlockSpec(memory_space=pltpu.VMEM)
    return pl.pallas_call(
        functools.partial(block_kernel, n_rows, n_cols),
        out_shape=pltpu.VMEM(patches.shape, bf16),
        in_specs=[pl.BlockSpec(memory_space=pltpu.HBM)] * len(args),
        out_specs=vmem,
        scratch_shapes=[pltpu.VMEM(a.shape, a.dtype) for a in args]
        + [
            pltpu.VMEM(big, bf16),
            pltpu.VMEM(big, bf16),
            pltpu.VMEM((tokens, states), bf16),
            pltpu.VMEM((tokens, states), bf16),
            pltpu.VMEM((states, tokens), bf16),
            pltpu.VMEM(big, bf16),
            pltpu.VMEM(big, f32),
            pltpu.VMEM(big, f32),
            pltpu.VMEM(big, f32),
            pltpu.VMEM(piece, bf16),
            pltpu.VMEM(piece, bf16),
            pltpu.VMEM((chunks, states, feats), f32),
            pltpu.VMEM((chunks, 1, feats), f32),
            pltpu.VMEM((chunks, states, feats), bf16),
            pltpu.VMEM((chunks, states, feats), bf16),
            pltpu.VMEM(piece, bf16),
            pltpu.VMEM(piece, bf16),
            pltpu.VMEM(piece, bf16),
            pltpu.VMEM(piece, bf16),
            pltpu.SemaphoreType.DMA((stages * (HALVES + 1), members)),
            pltpu.SemaphoreType.DMA((stages * (HALVES + 1), members)),
            pltpu.SemaphoreType.DMA((2, HALVES)),
            pltpu.VMEM(down, bf16),
            pltpu.VMEM(down, bf16),
            pltpu.SemaphoreType.DMA((2, stages)),
            pltpu.SemaphoreType.DMA((len(args) + HALVES,)),
        ],
        compiler_params=pltpu.CompilerParams(
            collective_id=0, has_side_effects=True, vmem_limit_bytes=56 * 1024 * 1024
        ),
    )(*args)


def solution(mesh):
    rep = P()
    return jax.shard_map(
        functools.partial(on_device, mesh.shape["rows"], mesh.shape["cols"]),
        mesh=mesh,
        in_specs=(P("rows", "cols", None), P("rows", "cols")) + (rep,) * 13,
        out_specs=P("rows", "cols", None),
        check_vma=False,
    )
```

```python
import functools

import jax
import jax.numpy as jnp
from jax import lax
from jax.experimental import pallas as pl
from jax.experimental.pallas import tpu as pltpu
from jax.sharding import PartitionSpec as P

MESH = pl.DeviceIdType.MESH
GROUPS = 2
MOST_STAGES = 2
HALVES = 2
f32 = jnp.float32
bf16 = jnp.bfloat16


def mm(a, b):
    return jnp.dot(a, b, preferred_element_type=f32)


def mm_nt(a, b):
    return lax.dot_general(a, b, (((1,), (1,)), ((), ())), preferred_element_type=f32)


def mm_tn(a, b):
    return lax.dot_general(a, b, (((0,), (0,)), ((), ())), preferred_element_type=f32)


def parts_of(x):
    high = x.astype(bf16)
    return high, (x - high.astype(f32)).astype(bf16)


def mm_split_right(a, x):
    high, low = parts_of(x)
    return mm(a, high) + mm(a, low)


def mm_split_left(x, b):
    high, low = parts_of(x)
    return mm(high, b) + mm(low, b)


def iota(shape, dim):
    return lax.broadcasted_iota(jnp.int32, shape, dim)


def log2_of(size):
    assert size & (size - 1) == 0
    return size.bit_length() - 1


def one_hot(index):
    count, lanes = index.shape
    lane = iota(index.shape, 1)
    tiles = [
        jnp.where(index - start == lane, 1.0, 0.0).astype(bf16)
        for start in range(0, count, lanes)
    ]
    return jnp.concatenate(tiles, axis=1)


ARGS = (
    "patches",
    "tissue",
    "w_value",
    "w_across",
    "w_down",
    "w_gate",
    "w_out",
    "bias_a",
    "bias_d",
    "rates_a",
    "rates_d",
    "skip_a",
    "skip_d",
    "gain_a",
    "gain_f",
)
SMALL = ARGS[7:]
LOAD_ORDER = ("tissue", "patches", "w_value", "w_across") + SMALL + ("w_gate", "w_down", "w_out")


def block_kernel(
    n_rows,
    n_cols,
    *refs,
):
    count = len(ARGS)
    sources, out_ref, held = refs[:count], refs[count], refs[count + 1 : 2 * count + 1]
    (
        masked,
        vals,
        b_all,
        c_all,
        bt_all,
        v_all,
        l_exp,
        y_all,
        gated,
        ordered,
        mixed_all,
        pushed_all,
        l_end,
        state_out,
        state_in,
        send1,
        recv1,
        send2,
        recv2,
        send_sems,
        recv_sems,
        relay_sems,
        down_out,
        down_in,
        down_sems,
        load_sems,
    ) = refs[2 * count + 1 :]
    loads = {
        name: pltpu.make_async_copy(sources[k], held[k], load_sems.at[k])
        for k, name in enumerate(ARGS)
        if name != "patches"
    }
    half_rows = sources[0].shape[0] // HALVES
    patch_loads = [
        pltpu.make_async_copy(
            sources[0].at[pl.ds(h * half_rows, half_rows)],
            held[0].at[pl.ds(h * half_rows, half_rows)],
            load_sems.at[count + h],
        )
        for h in range(HALVES)
    ]
    for name in LOAD_ORDER:
        if name == "patches":
            for load in patch_loads:
                load.start()
        else:
            loads[name].start()
    (
        patches_ref,
        tissue_ref,
        w_value_ref,
        w_across_ref,
        w_down_ref,
        w_gate_ref,
        w_out_ref,
        bias_a_ref,
        bias_d_ref,
        rates_a_ref,
        rates_d_ref,
        skip_a_ref,
        skip_d_ref,
        gain_a_ref,
        gain_f_ref,
    ) = held
    local_rows, width, feats = patches_ref.shape
    heads = rates_a_ref.shape[1]
    head_width = feats // heads
    states = (w_across_ref.shape[0] - heads) // 2
    tokens = local_rows * width
    chunk = width
    chunks = tokens // chunk
    members = n_rows // GROUPS
    per_peer = width // members
    height = members * local_rows
    stages = min(MOST_STAGES, per_peer)
    stage_tokens = tokens // stages
    stage_chunks = chunks // stages
    half_tokens = tokens // HALVES
    stage_lines = per_peer // stages
    per_line = height // chunk
    assert head_width == chunk and height % chunk == 0

    my_row = lax.axis_index("rows")
    my_col = lax.axis_index("cols")

    barrier = pltpu.get_barrier_semaphore()

    group_of = my_row // members
    member = lax.rem(my_row, members)
    base = group_of * members

    def fellow(off):
        return lax.rem(member + off, members)

    def each_fellow(body):
        if members <= 8:
            for off in range(1, members):
                body(off)
        else:
            pl.loop(1, members)(body)

    @each_fellow
    def _(off):
        pl.semaphore_signal(
            barrier, inc=1, device_id=(base + fellow(off), my_col), device_id_type=MESH
        )

    @pl.when(group_of > 0)
    def _():
        pl.semaphore_signal(
            barrier, inc=1, device_id=(my_row - members, my_col), device_id_type=MESH
        )

    @pl.when(my_col > 0)
    def _():
        pl.semaphore_signal(
            barrier, inc=1, device_id=(my_row, my_col - 1), device_id_type=MESH
        )

    lane = iota((heads, feats), 1)
    first = iota((heads, feats), 0) * head_width
    expand = jnp.where((lane >= first) & (lane < first + head_width), 1.0, 0.0).astype(bf16)
    place_t = iota((chunk, feats), 0)
    place_u = iota((chunk, feats), 1) & (head_width - 1)
    causal = place_t >= place_u
    diagonal = place_t == place_u
    pair = 2 if stage_chunks % 2 == 0 else 1
    span = pair * chunk
    tri_t, tri_u = iota((span, span), 0), iota((span, span), 1)
    csh = log2_of(chunk)
    tri = jnp.where(
        (tri_t >= tri_u)
        & (lax.shift_right_logical(tri_t, csh) == lax.shift_right_logical(tri_u, csh)),
        1.0,
        0.0,
    ).astype(bf16)
    tri = jnp.concatenate([tri, tri], axis=1)
    group = min(heads, 4)
    gw = group * head_width
    sh = log2_of(head_width)
    same_head = jnp.where(
        lax.shift_right_logical(iota((gw, gw), 0), sh)
        == lax.shift_right_logical(iota((gw, gw), 1), sh),
        1.0,
        0.0,
    ).astype(bf16)

    def wide(ref):
        return mm_split_left(jnp.broadcast_to(ref[...], (8, heads)), expand)[0:1]

    def tall(ref):
        square = jnp.broadcast_to(ref[...], (heads, heads))
        eye = iota((heads, heads), 0) == iota((heads, heads), 1)
        return jnp.sum(jnp.where(eye, square, 0.0), axis=1, keepdims=True)

    def spread(x):
        high, low = parts_of(x)
        return mm_tn(
            jnp.concatenate([high, low], axis=0), jnp.concatenate([expand, expand], axis=0)
        )

    def project(x, w_ref, bias, neg_rates, start=0):
        here = slice(start, start + x.shape[0])
        weights = w_ref[...]
        proj = mm_nt(x, weights[: 2 * states])
        b_all[here, :] = proj[:, :states].astype(bf16)
        c_all[here, :] = proj[:, states:].astype(bf16)
        turned = mm_nt(weights, x)
        bt_all[:, here] = turned[:states].astype(bf16)
        v = turned[2 * states :] + bias
        steps = jnp.maximum(v, 0.0) + jnp.log1p(jnp.exp(-jnp.abs(v)))
        v_all[here, :] = (spread(steps) * vals[here, :].astype(f32)).astype(bf16)
        high, low = parts_of(spread(steps * neg_rates))
        for g in range(0, x.shape[0], span):
            rows = slice(g, g + span)
            l_exp[start + g : start + g + span, :] = mm(tri, jnp.concatenate([high[rows], low[rows]], axis=0))

    def push(g):
        rows = slice(g * chunk, (g + 1) * chunk)
        run = l_exp[rows, :]
        end = run[chunk - 1 : chunk, :]
        scaled = v_all[rows, :].astype(f32) * jnp.exp(end - run)
        return end, mm(bt_all[:, rows], scaled.astype(bf16))

    def within(g, skips):
        rows = slice(g * chunk, (g + 1) * chunk)
        run = l_exp[rows, :]
        run_u = jnp.sum(jnp.where(diagonal, run, 0.0), axis=0, keepdims=True)
        b = b_all[rows, :]
        cb = mm_nt(c_all[rows, :], jnp.concatenate([b, b], axis=0))
        cb = jnp.concatenate([cb] * (heads // 2), axis=1)
        decay = jnp.exp(jnp.where(causal, run - run_u, -1e30))
        weights = (decay * cb).astype(bf16)
        vb = v_all[rows, :]
        outs = []
        for q in range(heads // group):
            lanes = slice(q * gw, (q + 1) * gw)
            stacked = jnp.concatenate([vb[:, lanes]] * group, axis=0) * same_head
            outs.append(mm(weights[:, lanes], stacked))
        return jnp.concatenate(outs, axis=1) + skips * vals[rows, :].astype(f32)

    def exchange(source, target, sems, part):
        def copy_of(off, to, place):
            return pltpu.make_async_remote_copy(
                src_ref=source.at[(to,) + part],
                dst_ref=target.at[(place,) + part],
                send_sem=send_sems.at[sems, off],
                recv_sem=recv_sems.at[sems, off],
                device_id=(base + to, my_col),
                device_id_type=MESH,
            )

        def start():
            @each_fellow
            def _(off):
                copy_of(off, fellow(off), member).start()

            target[(member,) + part] = source[(member,) + part]

        def finish():
            @each_fellow
            def _(off):
                came = fellow(members - off)
                copy_of(off, came, came).wait_recv()

        def drain():
            @each_fellow
            def _(off):
                copy_of(off, fellow(off), member).wait_send()

        return start, finish, drain

    def shaped(x, shape):
        if shape[-2] % 16:
            return x.astype(f32).reshape(shape).astype(bf16)
        return x.astype(bf16).reshape(shape)

    def flat(x):
        if x.shape[-2] % 16:
            return x.astype(f32).reshape(-1, feats).astype(bf16)
        return x.reshape(-1, feats)

    rsh = log2_of(half_rows)
    hsh = log2_of(height)
    lsh = log2_of(stage_lines)
    msh = log2_of(members)
    shr = lax.shift_right_logical
    m = iota((half_tokens, 128), 0)
    by_col = one_hot(
        ((m & (half_rows - 1)) << csh)
        + ((shr(m, rsh + lsh) & (members - 1)) << log2_of(per_peer))
        + (shr(m, rsh + lsh + msh) << lsh)
        + (shr(m, rsh) & (stage_lines - 1))
    )
    m = iota((stage_tokens, 128), 0)
    i_of = m & (height - 1)
    to_columns = one_hot(
        (shr(i_of, rsh) << (rsh + lsh)) + (shr(m, hsh) << rsh) + (i_of & (half_rows - 1))
    )

    def half(h):
        return slice(h * half_tokens, (h + 1) * half_tokens)

    def out_order(ref, h, x):
        x = mm(by_col, x)
        ref[:, :, h] = shaped(x, (stages, members) + ref.shape[3:])

    loads["tissue"].wait()
    flags = tissue_ref[...].astype(f32).T
    for name in ("w_value", "w_across") + SMALL:
        loads[name].wait()
    bias_a, neg_rates_a = tall(bias_a_ref), -tall(rates_a_ref)
    relays = [
        pltpu.make_async_remote_copy(
            src_ref=state_out.at[pl.ds(h * half_rows, half_rows)],
            dst_ref=state_in.at[pl.ds(h * half_rows, half_rows)],
            send_sem=relay_sems.at[0, h],
            recv_sem=relay_sems.at[1, h],
            device_id=(my_row, lax.rem(my_col + 1, n_cols)),
            device_id_type=MESH,
        )
        for h in range(HALVES)
    ]

    def rows_of(h):
        return range(h * half_rows, (h + 1) * half_rows)

    greeted = (
        members
        - 1
        + jnp.where(my_col < n_cols - 1, 1, 0)
        + jnp.where(group_of < GROUPS - 1, 1, 0)
    )

    @pl.when(my_col == 0)
    def _():
        state_in[...] = jnp.zeros_like(state_in)

    for h in range(HALVES):
        patch_loads[h].wait()
        for r in rows_of(h):
            flag = jnp.broadcast_to(flags[:, r : r + 1], (width, feats)) > 0.5
            masked[r * width : (r + 1) * width, :] = jnp.where(
                flag, patches_ref[r].astype(f32), 0.0
            ).astype(bf16)
        x = masked[half(h), :]
        vals[half(h), :] = mm(x, w_value_ref[...]).astype(bf16)
        project(x, w_across_ref, bias_a, neg_rates_a, h * half_tokens)

        @pl.when(my_col < n_cols - 1)
        def _():
            for g in rows_of(h):
                end, pushed = push(g)
                state_out[g] = pushed.astype(bf16)
                if n_cols > 2:
                    l_end[g], pushed_all[g] = end, pushed

        if h == 0:
            pl.semaphore_wait(barrier, greeted)

        if n_cols > 1:

            @pl.when(my_col == 0)
            def _():
                relays[h].start()

    skips = wide(skip_a_ref)

    for g in range(chunks):
        y_all[g * chunk : (g + 1) * chunk, :] = within(g, skips)

    def pass_on(h):
        @pl.when(my_col < n_cols - 1)
        def _():
            for g in rows_of(h):
                state_out[g] = (
                    pushed_all[g] + jnp.exp(l_end[g]) * state_in[g].astype(f32)
                ).astype(bf16)
            relays[h].start()

    gain_a = gain_a_ref[...]
    across = [
        [exchange(send1.at[k], recv1.at[k], k * HALVES + h, (h,)) for k in range(stages)]
        for h in range(HALVES)
    ]
    for h in range(HALVES):

        @pl.when(my_col > 0)
        def _():
            relays[h].wait_recv()

            if n_cols > 2:
                pass_on(h)

        parts = []
        for g in rows_of(h):
            rows = slice(g * chunk, (g + 1) * chunk)
            y = y_all[rows, :] + mm(c_all[rows, :], state_in[g]) * jnp.exp(l_exp[rows, :])
            scale = lax.rsqrt(jnp.mean(y * y, axis=-1, keepdims=True) + 1e-5)
            parts.append((y * scale * gain_a).astype(bf16))
        out_order(send1, h, jnp.concatenate(parts, axis=0))
        for k in range(stages):
            across[h][k][0]()

    for h in range(HALVES):
        out_order(ordered, h, masked[half(h), :])
    loads["w_gate"].wait()
    for k in range(stages):
        gate = mm(flat(ordered[k]), w_gate_ref[...])
        gated[k * stage_tokens : (k + 1) * stage_tokens, :] = (
            gate / (1.0 + jnp.exp(-gate)) * gain_f_ref[...]
        )
    skips_d = wide(skip_d_ref)
    bias_d, neg_rates_d = tall(bias_d_ref), -tall(rates_d_ref)
    loads["w_down"].wait()
    loads["w_out"].wait()

    @pl.when(my_col < n_cols - 1)
    def _():
        for copy in relays:
            copy.wait_send()

    hand_down = [
        pltpu.make_async_remote_copy(
            src_ref=down_out.at[k],
            dst_ref=down_in.at[k],
            send_sem=down_sems.at[0, k],
            recv_sem=down_sems.at[1, k],
            device_id=(lax.rem(my_row + members, n_rows), my_col),
            device_id_type=MESH,
        )
        for k in range(stages)
    ]

    @pl.when(group_of == 0)
    def _():
        down_in[...] = jnp.zeros_like(down_in)

    def ends(k):
        for c in range(stage_lines):
            entered = None
            for i in range(per_line):
                g = k * stage_chunks + c * per_line + i
                end, pushed = push(g)
                if per_line > 1:
                    l_end[g], pushed_all[g] = end, pushed
                entered = pushed if entered is None else jnp.exp(end) * entered + pushed
            down_out[k, c] = entered.astype(bf16)

    for k in range(stages):
        for h in range(HALVES):
            across[h][k][1]()
        first_token = k * stage_tokens
        cols = mm(to_columns, flat(recv1[k])).astype(bf16)
        vals[first_token : first_token + stage_tokens, :] = cols
        project(cols, w_down_ref, bias_d, neg_rates_d, first_token)
        if per_line > 1:
            ends(k)

        @pl.when(group_of < GROUPS - 1)
        def _():
            if per_line == 1:
                ends(k)
            hand_down[k].start()

    for g in range(chunks):
        y_all[g * chunk : (g + 1) * chunk, :] = within(g, skips_d)

    back = [exchange(send2.at[k], recv2.at[k], stages * HALVES + k, ()) for k in range(stages)]
    for k in range(stages):

        @pl.when(group_of > 0)
        def _():
            hand_down[k].wait_recv()

        parts = []
        for c in range(stage_lines):
            entered = down_in[k, c].astype(f32)
            for i in range(per_line):
                g = k * stage_chunks + c * per_line + i
                rows = slice(g * chunk, (g + 1) * chunk)
                extra = mm(c_all[rows, :], entered.astype(bf16)) * jnp.exp(l_exp[rows, :])
                parts.append((y_all[rows, :] + extra).astype(bf16))
                if i < per_line - 1:
                    entered = jnp.exp(l_end[g]) * entered + pushed_all[g]
        send2[k] = shaped(mm_tn(to_columns, jnp.concatenate(parts, axis=0)), send2.shape[1:])
        back[k][0]()

    for k in range(stages):
        back[k][1]()
        z = flat(recv2[k]).astype(f32)
        scale = lax.rsqrt(jnp.mean(z * z, axis=-1, keepdims=True) + 1e-5)
        act = z * scale * gated[k * stage_tokens : (k + 1) * stage_tokens, :]
        mixed = flat(ordered[k]).astype(f32) + mm(act.astype(bf16), w_out_ref[...])
        mixed_all[k] = shaped(mixed, mixed_all.shape[1:])
    for h in range(HALVES):
        mixed = mm_tn(by_col, flat(mixed_all[:, :, h])).astype(bf16)
        out_ref[h * half_rows : (h + 1) * half_rows] = mixed.reshape(half_rows, width, feats)

    for h in range(HALVES):
        for k in range(stages):
            across[h][k][2]()

    @pl.when(group_of < GROUPS - 1)
    def _():
        for copy in hand_down:
            copy.wait_send()

    for _, _, drain in back:
        drain()


def on_device(n_rows, n_cols, *args):
    args = [a.reshape(1, -1) if a.ndim == 1 else a for a in args]
    args[3], args[4] = args[3].T, args[4].T
    patches = args[0]
    local_rows, width, feats = patches.shape
    tokens = local_rows * width
    heads = args[9].shape[1]
    states = (args[3].shape[0] - heads) // 2
    chunks = local_rows
    members = n_rows // GROUPS
    stages = min(MOST_STAGES, width // members)
    stage_lines = width // members // stages
    piece = (stages, members, HALVES, local_rows // HALVES * stage_lines, feats)
    down = (stages, stage_lines, states, feats)
    big = (tokens, feats)
    vmem = pl.BlockSpec(memory_space=pltpu.VMEM)
    return pl.pallas_call(
        functools.partial(block_kernel, n_rows, n_cols),
        out_shape=pltpu.VMEM(patches.shape, bf16),
        in_specs=[pl.BlockSpec(memory_space=pltpu.HBM)] * len(args),
        out_specs=vmem,
        scratch_shapes=[pltpu.VMEM(a.shape, a.dtype) for a in args]
        + [
            pltpu.VMEM(big, bf16),
            pltpu.VMEM(big, bf16),
            pltpu.VMEM((tokens, states), bf16),
            pltpu.VMEM((tokens, states), bf16),
            pltpu.VMEM((states, tokens), bf16),
            pltpu.VMEM(big, bf16),
            pltpu.VMEM(big, f32),
            pltpu.VMEM(big, f32),
            pltpu.VMEM(big, f32),
            pltpu.VMEM(piece, bf16),
            pltpu.VMEM(piece, bf16),
            pltpu.VMEM((chunks, states, feats), f32),
            pltpu.VMEM((chunks, 1, feats), f32),
            pltpu.VMEM((chunks, states, feats), bf16),
            pltpu.VMEM((chunks, states, feats), bf16),
            pltpu.VMEM(piece, bf16),
            pltpu.VMEM(piece, bf16),
            pltpu.VMEM(piece, bf16),
            pltpu.VMEM(piece, bf16),
            pltpu.SemaphoreType.DMA((stages * (HALVES + 1), members)),
            pltpu.SemaphoreType.DMA((stages * (HALVES + 1), members)),
            pltpu.SemaphoreType.DMA((2, HALVES)),
            pltpu.VMEM(down, bf16),
            pltpu.VMEM(down, bf16),
            pltpu.SemaphoreType.DMA((2, stages)),
            pltpu.SemaphoreType.DMA((len(args) + HALVES,)),
        ],
        compiler_params=pltpu.CompilerParams(
            collective_id=0, has_side_effects=True, vmem_limit_bytes=56 * 1024 * 1024
        ),
    )(*args)


def solution(mesh):
    rep = P()
    return jax.shard_map(
        functools.partial(on_device, mesh.shape["rows"], mesh.shape["cols"]),
        mesh=mesh,
        in_specs=(P("rows", "cols", None), P("rows", "cols")) + (rep,) * 13,
        out_specs=P("rows", "cols", None),
        check_vma=False,
    )
```

```python
import functools

import jax
import jax.numpy as jnp
from jax import lax
from jax.experimental import pallas as pl
from jax.experimental.pallas import tpu as pltpu
from jax.sharding import PartitionSpec as P

MESH = pl.DeviceIdType.MESH
GROUPS = 2
MOST_STAGES = 4
HALVES = 1
f32 = jnp.float32
bf16 = jnp.bfloat16


def mm(a, b):
    return jnp.dot(a, b, preferred_element_type=f32)


def mm_nt(a, b):
    return lax.dot_general(a, b, (((1,), (1,)), ((), ())), preferred_element_type=f32)


def mm_tn(a, b):
    return lax.dot_general(a, b, (((0,), (0,)), ((), ())), preferred_element_type=f32)


def parts_of(x):
    high = x.astype(bf16)
    return high, (x - high.astype(f32)).astype(bf16)


def mm_split_right(a, x):
    high, low = parts_of(x)
    return mm(a, high) + mm(a, low)


def mm_split_left(x, b):
    high, low = parts_of(x)
    return mm(high, b) + mm(low, b)


def iota(shape, dim):
    return lax.broadcasted_iota(jnp.int32, shape, dim)


def log2_of(size):
    assert size & (size - 1) == 0
    return size.bit_length() - 1


def one_hot(index):
    count, lanes = index.shape
    lane = iota(index.shape, 1)
    tiles = [
        jnp.where(index - start == lane, 1.0, 0.0).astype(bf16)
        for start in range(0, count, lanes)
    ]
    return jnp.concatenate(tiles, axis=1)


ARGS = (
    "patches",
    "tissue",
    "w_value",
    "w_across",
    "w_down",
    "w_gate",
    "w_out",
    "bias_a",
    "bias_d",
    "rates_a",
    "rates_d",
    "skip_a",
    "skip_d",
    "gain_a",
    "gain_f",
)
SMALL = ARGS[7:]
LOAD_ORDER = ("tissue", "patches", "w_value", "w_across") + SMALL + ("w_gate", "w_down", "w_out")


def block_kernel(
    n_rows,
    n_cols,
    *refs,
):
    count = len(ARGS)
    sources, out_ref, held = refs[:count], refs[count], refs[count + 1 : 2 * count + 1]
    (
        masked,
        vals,
        b_all,
        c_all,
        bt_all,
        v_all,
        l_exp,
        y_all,
        gated,
        ordered,
        mixed_all,
        pushed_all,
        l_end,
        state_out,
        state_in,
        send1,
        recv1,
        send2,
        recv2,
        send_sems,
        recv_sems,
        relay_sems,
        down_out,
        down_in,
        down_sems,
        load_sems,
    ) = refs[2 * count + 1 :]
    loads = {
        name: pltpu.make_async_copy(sources[k], held[k], load_sems.at[k])
        for k, name in enumerate(ARGS)
        if name != "patches"
    }
    half_rows = sources[0].shape[0] // HALVES
    patch_loads = [
        pltpu.make_async_copy(
            sources[0].at[pl.ds(h * half_rows, half_rows)],
            held[0].at[pl.ds(h * half_rows, half_rows)],
            load_sems.at[count + h],
        )
        for h in range(HALVES)
    ]
    for name in LOAD_ORDER:
        if name == "patches":
            for load in patch_loads:
                load.start()
        else:
            loads[name].start()
    (
        patches_ref,
        tissue_ref,
        w_value_ref,
        w_across_ref,
        w_down_ref,
        w_gate_ref,
        w_out_ref,
        bias_a_ref,
        bias_d_ref,
        rates_a_ref,
        rates_d_ref,
        skip_a_ref,
        skip_d_ref,
        gain_a_ref,
        gain_f_ref,
    ) = held
    local_rows, width, feats = patches_ref.shape
    heads = rates_a_ref.shape[1]
    head_width = feats // heads
    states = (w_across_ref.shape[0] - heads) // 2
    tokens = local_rows * width
    chunk = width
    chunks = tokens // chunk
    members = n_rows // GROUPS
    per_peer = width // members
    height = members * local_rows
    stages = min(MOST_STAGES, per_peer)
    stage_tokens = tokens // stages
    stage_chunks = chunks // stages
    half_tokens = tokens // HALVES
    stage_lines = per_peer // stages
    per_line = height // chunk
    assert head_width == chunk and height % chunk == 0

    my_row = lax.axis_index("rows")
    my_col = lax.axis_index("cols")

    barrier = pltpu.get_barrier_semaphore()

    group_of = my_row // members
    member = lax.rem(my_row, members)
    base = group_of * members

    def fellow(off):
        return lax.rem(member + off, members)

    def each_fellow(body):
        if members <= 8:
            for off in range(1, members):
                body(off)
        else:
            pl.loop(1, members)(body)

    @each_fellow
    def _(off):
        pl.semaphore_signal(
            barrier, inc=1, device_id=(base + fellow(off), my_col), device_id_type=MESH
        )

    @pl.when(group_of > 0)
    def _():
        pl.semaphore_signal(
            barrier, inc=1, device_id=(my_row - members, my_col), device_id_type=MESH
        )

    @pl.when(my_col > 0)
    def _():
        pl.semaphore_signal(
            barrier, inc=1, device_id=(my_row, my_col - 1), device_id_type=MESH
        )

    lane = iota((heads, feats), 1)
    first = iota((heads, feats), 0) * head_width
    expand = jnp.where((lane >= first) & (lane < first + head_width), 1.0, 0.0).astype(bf16)
    place_t = iota((chunk, feats), 0)
    place_u = iota((chunk, feats), 1) & (head_width - 1)
    causal = place_t >= place_u
    diagonal = place_t == place_u
    pair = 2 if stage_chunks % 2 == 0 else 1
    span = pair * chunk
    tri_t, tri_u = iota((span, span), 0), iota((span, span), 1)
    csh = log2_of(chunk)
    tri = jnp.where(
        (tri_t >= tri_u)
        & (lax.shift_right_logical(tri_t, csh) == lax.shift_right_logical(tri_u, csh)),
        1.0,
        0.0,
    ).astype(bf16)
    tri = jnp.concatenate([tri, tri], axis=1)
    group = min(heads, 4)
    gw = group * head_width
    sh = log2_of(head_width)
    same_head = jnp.where(
        lax.shift_right_logical(iota((gw, gw), 0), sh)
        == lax.shift_right_logical(iota((gw, gw), 1), sh),
        1.0,
        0.0,
    ).astype(bf16)

    def wide(ref):
        return mm_split_left(jnp.broadcast_to(ref[...], (8, heads)), expand)[0:1]

    def tall(ref):
        square = jnp.broadcast_to(ref[...], (heads, heads))
        eye = iota((heads, heads), 0) == iota((heads, heads), 1)
        return jnp.sum(jnp.where(eye, square, 0.0), axis=1, keepdims=True)

    def spread(x):
        high, low = parts_of(x)
        return mm_tn(
            jnp.concatenate([high, low], axis=0), jnp.concatenate([expand, expand], axis=0)
        )

    def project(x, w_ref, bias, neg_rates, start=0):
        here = slice(start, start + x.shape[0])
        weights = w_ref[...]
        proj = mm_nt(x, weights[: 2 * states])
        b_all[here, :] = proj[:, :states].astype(bf16)
        c_all[here, :] = proj[:, states:].astype(bf16)
        turned = mm_nt(weights, x)
        bt_all[:, here] = turned[:states].astype(bf16)
        v = turned[2 * states :] + bias
        steps = jnp.maximum(v, 0.0) + jnp.log1p(jnp.exp(-jnp.abs(v)))
        v_all[here, :] = (spread(steps) * vals[here, :].astype(f32)).astype(bf16)
        high, low = parts_of(spread(steps * neg_rates))
        for g in range(0, x.shape[0], span):
            rows = slice(g, g + span)
            l_exp[start + g : start + g + span, :] = mm(tri, jnp.concatenate([high[rows], low[rows]], axis=0))

    def push(g):
        rows = slice(g * chunk, (g + 1) * chunk)
        run = l_exp[rows, :]
        end = run[chunk - 1 : chunk, :]
        scaled = v_all[rows, :].astype(f32) * jnp.exp(end - run)
        return end, mm(bt_all[:, rows], scaled.astype(bf16))

    def within(g, skips):
        rows = slice(g * chunk, (g + 1) * chunk)
        run = l_exp[rows, :]
        run_u = jnp.sum(jnp.where(diagonal, run, 0.0), axis=0, keepdims=True)
        b = b_all[rows, :]
        cb = mm_nt(c_all[rows, :], jnp.concatenate([b, b], axis=0))
        cb = jnp.concatenate([cb] * (heads // 2), axis=1)
        decay = jnp.exp(jnp.where(causal, run - run_u, -1e30))
        weights = (decay * cb).astype(bf16)
        vb = v_all[rows, :]
        outs = []
        for q in range(heads // group):
            lanes = slice(q * gw, (q + 1) * gw)
            stacked = jnp.concatenate([vb[:, lanes]] * group, axis=0) * same_head
            outs.append(mm(weights[:, lanes], stacked))
        return jnp.concatenate(outs, axis=1) + skips * vals[rows, :].astype(f32)

    def exchange(source, target, sems, part):
        def copy_of(off, to, place):
            return pltpu.make_async_remote_copy(
                src_ref=source.at[(to,) + part],
                dst_ref=target.at[(place,) + part],
                send_sem=send_sems.at[sems, off],
                recv_sem=recv_sems.at[sems, off],
                device_id=(base + to, my_col),
                device_id_type=MESH,
            )

        def start():
            @each_fellow
            def _(off):
                copy_of(off, fellow(off), member).start()

            target[(member,) + part] = source[(member,) + part]

        def finish():
            @each_fellow
            def _(off):
                came = fellow(members - off)
                copy_of(off, came, came).wait_recv()

        def drain():
            @each_fellow
            def _(off):
                copy_of(off, fellow(off), member).wait_send()

        return start, finish, drain

    def shaped(x, shape):
        if shape[-2] % 16:
            return x.astype(f32).reshape(shape).astype(bf16)
        return x.astype(bf16).reshape(shape)

    def flat(x):
        if x.shape[-2] % 16:
            return x.astype(f32).reshape(-1, feats).astype(bf16)
        return x.reshape(-1, feats)

    rsh = log2_of(half_rows)
    hsh = log2_of(height)
    lsh = log2_of(stage_lines)
    msh = log2_of(members)
    shr = lax.shift_right_logical
    m = iota((half_tokens, 128), 0)
    by_col = one_hot(
        ((m & (half_rows - 1)) << csh)
        + ((shr(m, rsh + lsh) & (members - 1)) << log2_of(per_peer))
        + (shr(m, rsh + lsh + msh) << lsh)
        + (shr(m, rsh) & (stage_lines - 1))
    )
    m = iota((stage_tokens, 128), 0)
    i_of = m & (height - 1)
    to_columns = one_hot(
        (shr(i_of, rsh) << (rsh + lsh)) + (shr(m, hsh) << rsh) + (i_of & (half_rows - 1))
    )

    def half(h):
        return slice(h * half_tokens, (h + 1) * half_tokens)

    def out_order(ref, h, x):
        x = mm(by_col, x)
        ref[:, :, h] = shaped(x, (stages, members) + ref.shape[3:])

    loads["tissue"].wait()
    flags = tissue_ref[...].astype(f32).T
    for name in ("w_value", "w_across") + SMALL:
        loads[name].wait()
    bias_a, neg_rates_a = tall(bias_a_ref), -tall(rates_a_ref)
    relays = [
        pltpu.make_async_remote_copy(
            src_ref=state_out.at[pl.ds(h * half_rows, half_rows)],
            dst_ref=state_in.at[pl.ds(h * half_rows, half_rows)],
            send_sem=relay_sems.at[0, h],
            recv_sem=relay_sems.at[1, h],
            device_id=(my_row, lax.rem(my_col + 1, n_cols)),
            device_id_type=MESH,
        )
        for h in range(HALVES)
    ]

    def rows_of(h):
        return range(h * half_rows, (h + 1) * half_rows)

    greeted = (
        members
        - 1
        + jnp.where(my_col < n_cols - 1, 1, 0)
        + jnp.where(group_of < GROUPS - 1, 1, 0)
    )

    @pl.when(my_col == 0)
    def _():
        state_in[...] = jnp.zeros_like(state_in)

    for h in range(HALVES):
        patch_loads[h].wait()
        for r in rows_of(h):
            flag = jnp.broadcast_to(flags[:, r : r + 1], (width, feats)) > 0.5
            masked[r * width : (r + 1) * width, :] = jnp.where(
                flag, patches_ref[r].astype(f32), 0.0
            ).astype(bf16)
        x = masked[half(h), :]
        vals[half(h), :] = mm(x, w_value_ref[...]).astype(bf16)
        project(x, w_across_ref, bias_a, neg_rates_a, h * half_tokens)

        @pl.when(my_col < n_cols - 1)
        def _():
            for g in rows_of(h):
                end, pushed = push(g)
                state_out[g] = pushed.astype(bf16)
                if n_cols > 2:
                    l_end[g], pushed_all[g] = end, pushed

        if h == 0:
            pl.semaphore_wait(barrier, greeted)

        if n_cols > 1:

            @pl.when(my_col == 0)
            def _():
                relays[h].start()

    skips = wide(skip_a_ref)

    for g in range(chunks):
        y_all[g * chunk : (g + 1) * chunk, :] = within(g, skips)

    def pass_on(h):
        @pl.when(my_col < n_cols - 1)
        def _():
            for g in rows_of(h):
                state_out[g] = (
                    pushed_all[g] + jnp.exp(l_end[g]) * state_in[g].astype(f32)
                ).astype(bf16)
            relays[h].start()

    gain_a = gain_a_ref[...]
    across = [
        [exchange(send1.at[k], recv1.at[k], k * HALVES + h, (h,)) for k in range(stages)]
        for h in range(HALVES)
    ]
    for h in range(HALVES):

        @pl.when(my_col > 0)
        def _():
            relays[h].wait_recv()

            if n_cols > 2:
                pass_on(h)

        parts = []
        for g in rows_of(h):
            rows = slice(g * chunk, (g + 1) * chunk)
            y = y_all[rows, :] + mm(c_all[rows, :], state_in[g]) * jnp.exp(l_exp[rows, :])
            scale = lax.rsqrt(jnp.mean(y * y, axis=-1, keepdims=True) + 1e-5)
            parts.append((y * scale * gain_a).astype(bf16))
        out_order(send1, h, jnp.concatenate(parts, axis=0))
        for k in range(stages):
            across[h][k][0]()

    for h in range(HALVES):
        out_order(ordered, h, masked[half(h), :])
    loads["w_gate"].wait()
    for k in range(stages):
        gate = mm(flat(ordered[k]), w_gate_ref[...])
        gated[k * stage_tokens : (k + 1) * stage_tokens, :] = (
            gate / (1.0 + jnp.exp(-gate)) * gain_f_ref[...]
        )
    skips_d = wide(skip_d_ref)
    bias_d, neg_rates_d = tall(bias_d_ref), -tall(rates_d_ref)
    loads["w_down"].wait()
    loads["w_out"].wait()

    @pl.when(my_col < n_cols - 1)
    def _():
        for copy in relays:
            copy.wait_send()

    hand_down = [
        pltpu.make_async_remote_copy(
            src_ref=down_out.at[k],
            dst_ref=down_in.at[k],
            send_sem=down_sems.at[0, k],
            recv_sem=down_sems.at[1, k],
            device_id=(lax.rem(my_row + members, n_rows), my_col),
            device_id_type=MESH,
        )
        for k in range(stages)
    ]

    @pl.when(group_of == 0)
    def _():
        down_in[...] = jnp.zeros_like(down_in)

    def ends(k):
        for c in range(stage_lines):
            entered = None
            for i in range(per_line):
                g = k * stage_chunks + c * per_line + i
                end, pushed = push(g)
                if per_line > 1:
                    l_end[g], pushed_all[g] = end, pushed
                entered = pushed if entered is None else jnp.exp(end) * entered + pushed
            down_out[k, c] = entered.astype(bf16)

    for k in range(stages):
        for h in range(HALVES):
            across[h][k][1]()
        first_token = k * stage_tokens
        cols = mm(to_columns, flat(recv1[k])).astype(bf16)
        vals[first_token : first_token + stage_tokens, :] = cols
        project(cols, w_down_ref, bias_d, neg_rates_d, first_token)
        if per_line > 1:
            ends(k)

        @pl.when(group_of < GROUPS - 1)
        def _():
            if per_line == 1:
                ends(k)
            hand_down[k].start()

    for g in range(chunks):
        y_all[g * chunk : (g + 1) * chunk, :] = within(g, skips_d)

    back = [exchange(send2.at[k], recv2.at[k], stages * HALVES + k, ()) for k in range(stages)]
    for k in range(stages):

        @pl.when(group_of > 0)
        def _():
            hand_down[k].wait_recv()

        parts = []
        for c in range(stage_lines):
            entered = down_in[k, c].astype(f32)
            for i in range(per_line):
                g = k * stage_chunks + c * per_line + i
                rows = slice(g * chunk, (g + 1) * chunk)
                extra = mm(c_all[rows, :], entered.astype(bf16)) * jnp.exp(l_exp[rows, :])
                parts.append((y_all[rows, :] + extra).astype(bf16))
                if i < per_line - 1:
                    entered = jnp.exp(l_end[g]) * entered + pushed_all[g]
        send2[k] = shaped(mm_tn(to_columns, jnp.concatenate(parts, axis=0)), send2.shape[1:])
        back[k][0]()

    for k in range(stages):
        back[k][1]()
        z = flat(recv2[k]).astype(f32)
        scale = lax.rsqrt(jnp.mean(z * z, axis=-1, keepdims=True) + 1e-5)
        act = z * scale * gated[k * stage_tokens : (k + 1) * stage_tokens, :]
        mixed = flat(ordered[k]).astype(f32) + mm(act.astype(bf16), w_out_ref[...])
        mixed_all[k] = shaped(mixed, mixed_all.shape[1:])
    for h in range(HALVES):
        mixed = mm_tn(by_col, flat(mixed_all[:, :, h])).astype(bf16)
        out_ref[h * half_rows : (h + 1) * half_rows] = mixed.reshape(half_rows, width, feats)

    for h in range(HALVES):
        for k in range(stages):
            across[h][k][2]()

    @pl.when(group_of < GROUPS - 1)
    def _():
        for copy in hand_down:
            copy.wait_send()

    for _, _, drain in back:
        drain()


def on_device(n_rows, n_cols, *args):
    args = [a.reshape(1, -1) if a.ndim == 1 else a for a in args]
    args[3], args[4] = args[3].T, args[4].T
    patches = args[0]
    local_rows, width, feats = patches.shape
    tokens = local_rows * width
    heads = args[9].shape[1]
    states = (args[3].shape[0] - heads) // 2
    chunks = local_rows
    members = n_rows // GROUPS
    stages = min(MOST_STAGES, width // members)
    stage_lines = width // members // stages
    piece = (stages, members, HALVES, local_rows // HALVES * stage_lines, feats)
    down = (stages, stage_lines, states, feats)
    big = (tokens, feats)
    vmem = pl.BlockSpec(memory_space=pltpu.VMEM)
    return pl.pallas_call(
        functools.partial(block_kernel, n_rows, n_cols),
        out_shape=pltpu.VMEM(patches.shape, bf16),
        in_specs=[pl.BlockSpec(memory_space=pltpu.HBM)] * len(args),
        out_specs=vmem,
        scratch_shapes=[pltpu.VMEM(a.shape, a.dtype) for a in args]
        + [
            pltpu.VMEM(big, bf16),
            pltpu.VMEM(big, bf16),
            pltpu.VMEM((tokens, states), bf16),
            pltpu.VMEM((tokens, states), bf16),
            pltpu.VMEM((states, tokens), bf16),
            pltpu.VMEM(big, bf16),
            pltpu.VMEM(big, f32),
            pltpu.VMEM(big, f32),
            pltpu.VMEM(big, f32),
            pltpu.VMEM(piece, bf16),
            pltpu.VMEM(piece, bf16),
            pltpu.VMEM((chunks, states, feats), f32),
            pltpu.VMEM((chunks, 1, feats), f32),
            pltpu.VMEM((chunks, states, feats), bf16),
            pltpu.VMEM((chunks, states, feats), bf16),
            pltpu.VMEM(piece, bf16),
            pltpu.VMEM(piece, bf16),
            pltpu.VMEM(piece, bf16),
            pltpu.VMEM(piece, bf16),
            pltpu.SemaphoreType.DMA((stages * (HALVES + 1), members)),
            pltpu.SemaphoreType.DMA((stages * (HALVES + 1), members)),
            pltpu.SemaphoreType.DMA((2, HALVES)),
            pltpu.VMEM(down, bf16),
            pltpu.VMEM(down, bf16),
            pltpu.SemaphoreType.DMA((2, stages)),
            pltpu.SemaphoreType.DMA((len(args) + HALVES,)),
        ],
        compiler_params=pltpu.CompilerParams(
            collective_id=0, has_side_effects=True, vmem_limit_bytes=56 * 1024 * 1024
        ),
    )(*args)


def solution(mesh):
    rep = P()
    return jax.shard_map(
        functools.partial(on_device, mesh.shape["rows"], mesh.shape["cols"]),
        mesh=mesh,
        in_specs=(P("rows", "cols", None), P("rows", "cols")) + (rep,) * 13,
        out_specs=P("rows", "cols", None),
        check_vma=False,
    )
```
